128 devices in a mesh: shard: 8 (over z, core), ctx: 2 (over x_hi), tp: 8 (over x_lo, y).
Axes of the slice: x: 4 (x_hi: 2, x_lo: 2; x = x_hi * 2 + x_lo), y: 4, z: 4, core: 2. Of those that a mesh axis runs over, the one named last changes fastest.
Arguments:
- tokens: bfloat16 [8, 736, 1152], P('shard', 'ctx'), may hold values from -6 to 6
- image_count: int32 [8], P('shard'), may hold values from 0 to 1, as said below
- ln_gain: bfloat16 [2, 1152], P(None, 'shard'), may hold values from 0.25 to 1.75
- vec_bias: bfloat16 [4, 1152], P(None, 'shard'), may hold values from -3 to 3
- w_qkv: bfloat16 [3, 1152, 1152], P(None, 'shard', 'tp')
- qv_bias: bfloat16 [2, 1152], P(None, 'tp'), may hold values from -3 to 3
- w_out: bfloat16 [1152, 1152], P('tp', 'shard'), may hold values from -1.5 to 1.5
- w_fc1: bfloat16 [1152, 4304], P('shard', 'tp'), may hold values from -0.1875 to 0.1875
- fc1_bias: bfloat16 [4304], P('tp'), may hold values from -3 to 3
- w_fc2: bfloat16 [4304, 1152], P('tp', 'shard'), may hold values from -0.09375 to 0.09375
- cotangent: bfloat16 [8, 736, 1152], P('shard', 'ctx'), may hold values from -6 to 6
Outputs:
- layer_out: bfloat16 [8, 736, 1152], P('shard', 'ctx')
- grad_tokens: float32 [8, 736, 1152], P('shard', 'ctx')
- grad_ln_gain: float32 [2, 1152], P(None, 'shard')
- grad_vec_bias: float32 [4, 1152], P(None, 'shard')
- grad_qkv: float32 [3, 1152, 1152], P(None, 'shard', 'tp')
- grad_qv_bias: float32 [2, 1152], P(None, 'tp')
- grad_out: float32 [1152, 1152], P('tp', 'shard')
- grad_fc1: float32 [1152, 4304], P('shard', 'tp')
- grad_fc1_bias: float32 [4304], P('tp')
- grad_fc2: float32 [4304, 1152], P('tp', 'shard')
The draws below stay inside these ranges and needn't reach their ends.
Inputs may be any that keep to these rules, and one draw needn't show every extreme that they name: image_count[j] live images fill the first slots of index j of shard; some index holds 1 and some holds none.
All inputs are finite; a program needn't handle non-finite values.
Results may differ from the reference program's by a relative error of at most 0.009.
The reference program's roundings to bfloat16 on the way count: a program that leaves them out, or rounds other values in their place, can miss the bound.
Values may be sent and summed in bfloat16 or wider, within the bound.
A program may use at most 64 MiB of HBM per device.

```python
import math
import jax
import jax.numpy as jnp
from jax import lax

D = 1152
HEADS = 16
HD = 72
FF = 4304
IMG_TOK = 729
SLOTS = 1
POS = 736
SHARDS = 8
IMAGES = 8


def draw_image_count(key, part):
    key_one, key_two = jax.random.split(key)
    counts = jax.random.randint(key_one, (SHARDS,), 0, SLOTS + 1)
    shuffled = jax.random.permutation(key_two, SHARDS)
    return counts.at[shuffled[0]].set(SLOTS).at[shuffled[1]].set(0).astype(jnp.int32)


def draw_w_qkv(key, part):
    key_list = jax.random.split(key, 1)
    normal_base = jax.random.normal(key_list[0], (3, D, D), jnp.float32) * D ** (-0.5)
    stacked = normal_base
    return stacked.astype(jnp.bfloat16)


def block_scale(key, dims, shards, smallest, largest):
    loudness, own = 1.0, jax.random.fold_in(key, 6)
    for dim, shards_of in shards:
        heights = jnp.exp(jax.random.uniform(jax.random.fold_in(own, dim), (shards_of,), jnp.float32, smallest / len(shards), largest / len(shards)))
        loudness = loudness * jnp.repeat(heights, dims[dim] // shards_of).reshape([-1 if axis == dim else 1 for axis in range(len(dims))])
    return loudness


def bell_draw(key, shape, spread, most, shards=(), kind=jnp.bfloat16):
    factor_of = block_scale(key, shape, shards, -0.22, 0.18) if shards else 1.0
    values = jax.random.normal(key, shape, jnp.float32) * spread * factor_of
    return jnp.minimum(jnp.maximum(values, -most), most).astype(kind)


def setup_inputs(seed: int = 0) -> dict:
    arg_keys = jax.random.split(jax.random.key(seed), 12)
    return {
        "tokens": bell_draw(arg_keys[0], (IMAGES, POS, D), 1.0, 6.0, ((0, 8), (1, 2))),
        "image_count": draw_image_count(jax.random.fold_in(arg_keys[11], 71), 0),
        "ln_gain": jnp.clip(1.0 + 0.15 * jax.random.normal(arg_keys[2], (2, D), jnp.float32), 0.25, 1.75).astype(jnp.bfloat16),
        "vec_bias": bell_draw(arg_keys[3], (4, D), 0.5, 3.0, ((1, 8),)),
        "w_qkv": draw_w_qkv(jax.random.fold_in(arg_keys[11], 71), 0),
        "qv_bias": bell_draw(arg_keys[5], (2, D), 0.5, 3.0, ((1, 8),)),
        "w_out": bell_draw(arg_keys[6], (D, D), (max(D // 64, 1)) ** -0.5, 1.5, ((0, 8), (1, 8))),
        "w_fc1": bell_draw(arg_keys[7], (D, FF), D ** -0.5, 0.1875, ((0, 8), (1, 8))),
        "fc1_bias": bell_draw(arg_keys[8], (FF,), 0.5, 3.0, ((0, 8),)),
        "w_fc2": bell_draw(arg_keys[9], (FF, D), FF ** -0.5, 0.09375, ((0, 8), (1, 8))),
        "cotangent": bell_draw(arg_keys[10], (IMAGES, POS, D), 1.0, 6.0, ((0, 8), (1, 2))),
    }


EPS = 1e-06
GELU_C = math.sqrt(2.0 / math.pi)
GELU_A = 0.044715

def normalize(values_in, gain, shift):
    centre = lax.optimization_barrier(jnp.mean(values_in, axis=-1, keepdims=True))
    centred = values_in - centre
    variance = lax.optimization_barrier(jnp.mean(centred * centred, axis=-1, keepdims=True))
    inv_std = lax.rsqrt(variance + EPS)
    normed = centred * inv_std
    return (normed * gain + shift, normed, inv_std)

def norm_back(upstream, normed, inv_std, gain):
    scaled = upstream * gain
    return inv_std * (scaled - lax.optimization_barrier(jnp.mean(scaled, axis=-1, keepdims=True)) - normed * lax.optimization_barrier(jnp.mean(scaled * normed, axis=-1, keepdims=True)))

def gelu_tanh(inputs):
    inner = GELU_C * (inputs + GELU_A * inputs * inputs * inputs)
    return 0.5 * inputs * (1.0 + jnp.tanh(inner))

def gelu_slope(inputs):
    tangent = jnp.tanh(GELU_C * (inputs + GELU_A * inputs * inputs * inputs))
    return 0.5 * (1.0 + tangent) + 0.5 * inputs * (1.0 - tangent * tangent) * GELU_C * (1.0 + 3.0 * GELU_A * inputs * inputs)

def matmul(left, right):
    return jnp.dot(left, right, preferred_element_type=jnp.float32)

def rounded(values_in):
    return lax.optimization_barrier(values_in.astype(jnp.bfloat16))

def reference(tokens, image_count, ln_gain, vec_bias, w_qkv, qv_bias, w_out, w_fc1, fc1_bias, w_fc2, cotangent):
    score_scale = HD ** (-0.5)
    slot_live = jnp.tile(jnp.arange(SLOTS), SHARDS) < jnp.repeat(image_count, SLOTS)
    key_valid = jnp.arange(POS) < IMG_TOK
    gains = ln_gain.astype(jnp.float32)
    biases = vec_bias.astype(jnp.float32)
    qv_shift = qv_bias.astype(jnp.float32)
    fc1_shift = fc1_bias.astype(jnp.float32)

    def one_image(totals, inputs):
        image, upstream, alive = inputs
        row_mask = (key_valid & alive).astype(jnp.float32)[:, None]
        residual_in = image.astype(jnp.float32)
        normed_a, normed_one, inv_one = normalize(residual_in, gains[0], biases[0])
        attn_in = normed_a.astype(jnp.bfloat16)
        query = rounded(matmul(attn_in, w_qkv[0]) + qv_shift[0])
        keys_all = rounded(matmul(attn_in, w_qkv[1]))
        values_all = rounded(matmul(attn_in, w_qkv[2]) + qv_shift[1])
        query_heads = query.astype(jnp.float32).reshape(POS, HEADS, HD)
        key_heads = keys_all.astype(jnp.float32).reshape(POS, HEADS, HD)
        value_heads = values_all.astype(jnp.float32).reshape(POS, HEADS, HD)
        scores = jnp.einsum('phe,khe->hpk', query_heads, key_heads) * score_scale
        scores = jnp.where(key_valid[None, None, :], scores, -1e+30)
        row_peak = lax.optimization_barrier(jnp.max(scores, axis=-1, keepdims=True))
        log_total = row_peak + jnp.log(lax.optimization_barrier(jnp.sum(jnp.exp(scores - row_peak), axis=-1, keepdims=True)))
        attn_prob = jnp.exp(scores - log_total)
        prob_low = rounded(attn_prob).astype(jnp.float32)
        attended = rounded(jnp.einsum('hpk,khe->phe', prob_low, value_heads).reshape(POS, D))
        after_attn = residual_in + matmul(attended, w_out) + biases[2]
        normed_b, normed_two, inv_two = normalize(after_attn, gains[1], biases[1])
        mlp_in = normed_b.astype(jnp.bfloat16)
        hidden_pre = matmul(mlp_in, w_fc1) + fc1_shift
        hidden_act = gelu_tanh(hidden_pre).astype(jnp.bfloat16)
        layer_out = (after_attn + matmul(hidden_act, w_fc2) + biases[3]) * row_mask
        grad_y = upstream.astype(jnp.float32) * row_mask
        grad_low = grad_y.astype(jnp.bfloat16)
        grad_fc2 = matmul(hidden_act.T, grad_low)
        grad_pre = matmul(grad_low, w_fc2.T) * gelu_slope(hidden_pre)
        grad_fc1_bias = lax.optimization_barrier(jnp.sum(grad_pre, axis=0))
        grad_pre_bf = grad_pre.astype(jnp.bfloat16)
        grad_fc1 = matmul(mlp_in.T, grad_pre_bf)
        grad_mlp_in = matmul(grad_pre_bf, w_fc1.T)
        grad_after = grad_y + norm_back(grad_mlp_in, normed_two, inv_two, gains[1])
        grad_after_bf = grad_after.astype(jnp.bfloat16)
        grad_out = matmul(attended.T, grad_after_bf)
        grad_attended = rounded(matmul(grad_after_bf, w_out.T))
        grad_att_heads = grad_attended.astype(jnp.float32).reshape(POS, HEADS, HD)
        attended_heads = attended.astype(jnp.float32).reshape(POS, HEADS, HD)
        delta = lax.optimization_barrier(jnp.sum(grad_att_heads * attended_heads, axis=-1)).T[:, :, None]
        grad_prob = jnp.einsum('phe,khe->hpk', grad_att_heads, value_heads)
        grad_scores = rounded(attn_prob * (grad_prob - delta)).astype(jnp.float32)
        grad_query = jnp.einsum('hpk,khe->phe', grad_scores, key_heads).reshape(POS, D) * score_scale
        grad_keys = jnp.einsum('hpk,phe->khe', grad_scores, query_heads).reshape(POS, D) * score_scale
        grad_values = jnp.einsum('hpk,phe->khe', prob_low, grad_att_heads).reshape(POS, D)
        grad_qv_bias = jnp.stack([lax.optimization_barrier(jnp.sum(grad_query, axis=0)), lax.optimization_barrier(jnp.sum(grad_values, axis=0))])
        grad_parts = [grad_query.astype(jnp.bfloat16), grad_keys.astype(jnp.bfloat16), grad_values.astype(jnp.bfloat16)]
        grad_qkv = jnp.stack([matmul(attn_in.T, piece) for piece in grad_parts])
        grad_attn_in = matmul(grad_parts[0], w_qkv[0].T) + matmul(grad_parts[1], w_qkv[1].T) + matmul(grad_parts[2], w_qkv[2].T)
        grad_tokens = grad_after + norm_back(grad_attn_in, normed_one, inv_one, gains[0])
        grad_ln_gain = jnp.stack([lax.optimization_barrier(jnp.sum(grad_attn_in * normed_one, axis=0)), lax.optimization_barrier(jnp.sum(grad_mlp_in * normed_two, axis=0))])
        grad_vec_bias = jnp.stack([lax.optimization_barrier(jnp.sum(grad_attn_in, axis=0)), lax.optimization_barrier(jnp.sum(grad_mlp_in, axis=0)), lax.optimization_barrier(jnp.sum(grad_after, axis=0)), lax.optimization_barrier(jnp.sum(grad_y, axis=0))])
        updates = (grad_ln_gain, grad_vec_bias, grad_qkv, grad_qv_bias, grad_out, grad_fc1, grad_fc1_bias, grad_fc2)
        totals = tuple((total + piece for total, piece in zip(totals, updates)))
        return (totals, (layer_out.astype(jnp.bfloat16), grad_tokens))
    zeros_init = (jnp.zeros((2, D), jnp.float32), jnp.zeros((4, D), jnp.float32), jnp.zeros((3, D, D), jnp.float32), jnp.zeros((2, D), jnp.float32), jnp.zeros((D, D), jnp.float32), jnp.zeros((D, FF), jnp.float32), jnp.zeros((FF,), jnp.float32), jnp.zeros((FF, D), jnp.float32))
    totals, stacked = lax.scan(one_image, zeros_init, (tokens, cotangent, slot_live))
    layer_out, grad_tokens = stacked
    return (layer_out, grad_tokens, totals[0], totals[1], totals[2], totals[3], totals[4], totals[5], totals[6], totals[7])
```

```python
import math

import jax
import jax.numpy as jnp
from jax import lax
from jax.experimental import pallas as pl
from jax.experimental.pallas import tpu as pltpu
from jax.sharding import PartitionSpec as P

HD = 72
IMG_TOK = 729
EPS = 1e-06
GELU_C = math.sqrt(2.0 / math.pi)
GELU_A = 0.044715
SCALE = HD ** (-0.5)

D = 1152
ROWS = 368
PAD = 384
OWN = 48
BLK = 144
LN = 640
FF_OWN = 538
CH = 96

MESH = pl.DeviceIdType.MESH
F32 = jnp.float32
BF = jnp.bfloat16


def nn(a, b):
    return jnp.dot(a, b, preferred_element_type=F32)


def nt(a, b):
    return lax.dot_general(a, b, (((1,), (1,)), ((), ())), preferred_element_type=F32)


def tn(a, b):
    return lax.dot_general(a, b, (((0,), (0,)), ((), ())), preferred_element_type=F32)


def mean_rows(x):
    return jnp.sum(x, axis=-1, keepdims=True) * (1.0 / D)


def rcopy(src, dst, send, recv, dev):
    return pltpu.make_async_remote_copy(
        src_ref=src,
        dst_ref=dst,
        send_sem=send,
        recv_sem=recv,
        device_id=dev,
        device_id_type=MESH,
    )


def rows_at(start, size, unit=16):
    if not isinstance(start, int):
        start = pl.multiple_of(start, unit)
    return pl.ds(start, size)


def layer_kernel(
    count,
    tok,
    cot,
    wa_in,
    wb_in,
    wc_in,
    bias_rows,
    out_ref,
    gtok_ref,
    ga_ref,
    gb_ref,
    gc_ref,
    vec_ref,
    small_ref,
    wa,
    wb,
    wc,
    tokp,
    glow,
    attin,
    qh,
    kvo,
    kvx,
    sel,
    sela,
    prob,
    att,
    atth,
    part1,
    part2,
    part3,
    part4,
    rr1,
    rr2,
    rr3,
    rr4,
    g1,
    g2,
    g3,
    g4,
    gp0,
    hid,
    gpb,
    xh2,
    aft,
    r2s,
    gao,
    vrows,
    vecg,
    fulla,
    fullb,
    fullc,
    xs,
    xr,
    zs,
    zr,
    cs,
    cr,
    totb,
    dks,
    dkr,
    dkown,
    dqb,
    dsb,
    pbf,
    gah,
    gs,
    smx,
    smz,
    smc,
    vt,
    wz_s,
    wz_r,
    wc_s,
    wc_r,
    kv_s,
    kv_r,
    dk_s,
    dk_r,
    rs_s,
    rs_r,
    ag_s,
    ag_r,
    x_s,
    x_r,
    z_s,
    z_r,
    c_s,
    c_r,
    sx_s,
    sx_r,
    sz_s,
    sz_r,
    sc_s,
    sc_r,
    v_s,
    v_r,
):
    s = lax.axis_index("shard")
    c = lax.axis_index("ctx")
    t = lax.axis_index("tp")
    z = s // 2
    core = lax.rem(s, 2)
    sib = {"shard": z * 2 + 1 - core}
    octx = {"ctx": 1 - c}

    def zdev(zz):
        return {"shard": zz * 2 + core}

    def zoff(d):
        return lax.rem(z + d + 4, 4)

    def tpd(d):
        return lax.rem(t + d, 8)

    pending = []

    bar = pltpu.get_barrier_semaphore()
    for d in range(1, 8):
        pl.semaphore_signal(bar, inc=1, device_id={"tp": tpd(d)}, device_id_type=MESH)
    for d in range(1, 4):
        pl.semaphore_signal(bar, inc=1, device_id=zdev(zoff(d)), device_id_type=MESH)
    pl.semaphore_signal(bar, inc=1, device_id=sib, device_id_type=MESH)
    pl.semaphore_signal(bar, inc=1, device_id=octx, device_id_type=MESH)
    pl.semaphore_wait(bar, 12)

    groups = ((wa_in, wa), (wb_in, wb), (wc_in, wc))

    def block(ref, idx):
        return ref.at[rows_at(idx * BLK, BLK)]

    def w_start(g):
        src, full = groups[g]
        for d in (2, 1, 3):
            cp = rcopy(src, block(full, s), wz_s.at[g, d - 1], wz_r.at[g, d - 1], zdev(zoff(d)))
            cp.start()
            pending.append(cp)
        cp = rcopy(src, block(full, s), wc_s.at[g, 0], wc_r.at[g, 0], sib)
        cp.start()
        pending.append(cp)
        full[rows_at(s * BLK, BLK), :] = src[...]

    def w_forward(g):
        full = groups[g][1]
        for d in (1, 3, 2):
            got = block(full, zoff(-d) * 2 + core)
            rcopy(got, got, wz_s.at[g, d - 1], wz_r.at[g, d - 1], sib).wait_recv()
            cp = rcopy(got, got, wc_s.at[g, d], wc_r.at[g, d], sib)
            cp.start()
            pending.append(cp)

    def w_wait(g):
        full = groups[g][1]
        for d in range(4):
            got = block(full, zoff(-d) * 2 + 1 - core)
            rcopy(got, got, wc_s.at[g, d], wc_r.at[g, d], sib).wait_recv()

    w_start(0)

    def rs_send(k, part, rr, j):
        @pl.when(j != t)
        def _():
            rcopy(
                part.at[rows_at(j * OWN, OWN)], rr.at[t], rs_s.at[k, j], rs_r.at[k, t], {"tp": j}
            ).start()

    def rs_chunk(i):
        return lax.rem(t // 2 + 1 + i, 4)

    def rs_sum(k, part, rr):
        total = part[rows_at(t * OWN, OWN), :].astype(F32)
        for d in range(1, 8):
            j = tpd(d)
            rcopy(rr.at[j], rr.at[j], rs_s.at[k, j], rs_r.at[k, j], {"tp": j}).wait_recv()
            total = total + rr[j].astype(F32)
        return total

    def rs_done(k, part, rr):
        for d in range(1, 8):
            j = tpd(d)
            rcopy(
                part.at[rows_at(j * OWN, OWN)], rr.at[t], rs_s.at[k, j], rs_r.at[k, t], {"tp": j}
            ).wait_send()

    def ag_start(k, buf):
        mine = buf.at[rows_at(t * OWN, OWN)]
        for d in range(1, 8):
            cp = rcopy(mine, mine, ag_s.at[k, d], ag_r.at[k, t], {"tp": tpd(d)})
            cp.start()
            pending.append(cp)

    def ag_wait_block(k, buf, j):
        @pl.when(j != t)
        def _():
            blk = buf.at[rows_at(j * OWN, OWN)]
            rcopy(blk, blk, ag_s.at[k, 0], ag_r.at[k, j], {"tp": j}).wait_recv()

    def ag_wait(k, buf):
        for d in range(1, 8):
            j = tpd(d)
            blk = buf.at[rows_at(j * OWN, OWN)]
            rcopy(blk, blk, ag_s.at[k, 0], ag_r.at[k, j], {"tp": j}).wait_recv()

    row_i = lax.broadcasted_iota(jnp.int32, (128, 512), 0)
    lane_i = lax.broadcasted_iota(jnp.int32, (128, 512), 1)
    for j in range(6):
        hit = (lane_i == row_i + (16 + HD * j)) & (row_i < HD)
        sel[128 * j : 128 * j + 128, :] = jnp.where(hit, 1.0, 0.0).astype(BF)
    row_h = lax.broadcasted_iota(jnp.int32, (128, 256), 0)
    lane_h = lax.broadcasted_iota(jnp.int32, (128, 256), 1)
    for j in range(2):
        hit = (lane_h == row_h + HD * j) & (row_h < HD)
        sela[128 * j : 128 * j + 128, :] = jnp.where(hit, 1.0, 0.0).astype(BF)

    live = jnp.where(count[0] > 0, 1.0, 0.0)
    limit = IMG_TOK - c * ROWS

    def mask_at(start, size):
        pos = lax.broadcasted_iota(jnp.int32, (size, 1), 0) + start
        return jnp.where(pos < jnp.minimum(limit, ROWS), live, 0.0)

    def stats(x):
        centred = x - mean_rows(x)
        inv = lax.rsqrt(mean_rows(centred * centred) + EPS)
        return centred * inv, inv

    def prep(i, _):
        at = rows_at(i * 16, 16)
        tokp[at, :] = tok[at, :]
        glow[at, :] = (cot[at, :].astype(F32) * mask_at(i * 16, 16)).astype(BF)
        return 0

    lax.fori_loop(0, ROWS // 16, prep, 0)
    tokp[ROWS:PAD, :] = jnp.zeros((PAD - ROWS, D), BF)
    glow[ROWS:PAD, :] = jnp.zeros((PAD - ROWS, D), BF)
    vecg[...] = jnp.zeros_like(vecg)

    w_forward(0)
    w_wait(0)
    w_start(1)
    vrows[...] = wa[:, 512:640].astype(F32).T
    gain0 = vrows[64:65, :]
    gain1 = vrows[65:66, :]
    bias0 = vrows[66:67, :]
    bias1 = vrows[67:68, :]
    bias2 = vrows[68:69, :]
    bias3 = vrows[69:70, :]

    def norm_one(i, _):
        at = rows_at(i * 48, 48)
        normed, _inv = stats(tokp[at, :].astype(F32))
        attin[at, :] = (normed * gain0 + bias0).astype(BF)
        return 0

    lax.fori_loop(0, 8, norm_one, 0)

    def project(i, _):
        at = rows_at(i * 128, 128)
        low = (nn(attin[at, :], wa[:, 128:640]) + bias_rows[0:1, 0:512]).astype(BF)
        heads = nt(low, sel[...]).astype(BF)
        for j in range(2):
            qh[j, at, :] = heads[:, 128 * j : 128 * j + 128]
        for j in range(4):
            kvo[j, at, :] = heads[:, 256 + 128 * j : 384 + 128 * j]
        return 0

    lax.fori_loop(0, 3, project, 0)
    for j in range(4):
        cp = rcopy(kvo.at[j], kvx.at[j], kv_s.at[j], kv_r.at[j], octx)
        cp.start()
        pending.append(cp)

    lane_k = lax.broadcasted_iota(jnp.int32, (128, PAD), 1)
    own_keys = jnp.minimum(limit, ROWS)
    other_keys = jnp.minimum(IMG_TOK - (1 - c) * ROWS, ROWS)

    def own_scores(i, _):
        at = rows_at(i * 128, 128)
        for h in range(2):
            sc = nt(qh[h, at, :], kvo[h]) * SCALE
            prob[h, at, 0:PAD] = jnp.where(lane_k < own_keys, sc, -1e30)
        return 0

    lax.fori_loop(0, 3, own_scores, 0)
    w_forward(1)
    w_start(2)
    for j in range(4):
        rcopy(kvo.at[j], kvx.at[j], kv_s.at[j], kv_r.at[j], octx).wait_recv()

    def attend(i, _):
        at = rows_at(i * 128, 128)
        lows = []
        for h in range(2):
            sc = nt(qh[h, at, :], kvx[h]) * SCALE
            sc = jnp.where(lane_k < other_keys, sc, -1e30)
            so = prob[h, at, 0:PAD]
            peak = jnp.maximum(
                jnp.max(sc, axis=-1, keepdims=True), jnp.max(so, axis=-1, keepdims=True)
            )
            eo = jnp.exp(so - peak)
            ex = jnp.exp(sc - peak)
            inv = 1.0 / (
                jnp.sum(eo, axis=-1, keepdims=True) + jnp.sum(ex, axis=-1, keepdims=True)
            )
            po = eo * inv
            px = ex * inv
            prob[h, at, 0:PAD] = po
            prob[h, at, PAD : 2 * PAD] = px
            pol = po.astype(BF)
            pxl = px.astype(BF)
            pbf[h, at, 0:PAD] = pol
            pbf[h, at, PAD : 2 * PAD] = pxl
            low = (nn(pol, kvo[2 + h]) + nn(pxl, kvx[2 + h])).astype(BF)
            atth[h, at, :] = low
            lows.append(low)
        packed = nn(lows[0], sela[0:128, :]) + nn(lows[1], sela[128:256, :])
        att[at, :] = packed.astype(BF)
        return 0

    lax.fori_loop(0, 3, attend, 0)

    def out_proj(i, _):
        ch = rs_chunk(i)
        at = rows_at(ch * CH, CH)
        part1[at, :] = nt(att[at, :], wa[:, 0:256]).astype(BF)
        for b in range(2):
            rs_send(0, part1, rr1, ch * 2 + b)
        return 0

    lax.fori_loop(0, 4, out_proj, 0)
    w_wait(1)
    w_forward(2)
    w_wait(2)

    def fc2_back(i, _):
        at = rows_at(i * 128, 128)
        gp0[at, :] = nn(glow[at, :], wc[...])
        return 0

    lax.fori_loop(0, 3, fc2_back, 0)

    own = rows_at(t * OWN, OWN)
    after = tokp[own, :].astype(F32) + rs_sum(0, part1, rr1) + bias2
    aft[...] = after
    normed_two, inv_two = stats(after)
    xh2[...] = normed_two
    r2s[...] = jnp.broadcast_to(inv_two, (OWN, 128))
    g1[own, :] = (normed_two * gain1 + bias1).astype(BF)
    ag_start(0, g1)

    def mlp(i, colsum):
        ch = lax.rem(t // 2 + i, 4)
        at = rows_at(ch * CH, CH)
        for b in range(2):
            ag_wait_block(0, g1, ch * 2 + b)
        u = nn(g1[at, :], wb[...]) + bias_rows[1:2, :]
        uu = u * u
        tang = jnp.tanh(GELU_C * u * (1.0 + GELU_A * uu))
        hid[at, :] = (0.5 * u * (1.0 + tang)).astype(BF)
        slope = 0.5 * (1.0 + tang) + (0.5 * GELU_C) * u * (1.0 - tang * tang) * (
            1.0 + 3.0 * GELU_A * uu
        )
        gpre = gp0[at, :] * slope
        low = gpre.astype(BF)
        gpb[at, :] = low
        part2[at, :] = nt(low, wb[...]).astype(BF)
        for b in range(2):
            rs_send(1, part2, rr2, ch * 2 + b)
        return colsum + jnp.sum(gpre, axis=0, keepdims=True)

    fc1_sum = lax.fori_loop(0, 4, mlp, jnp.zeros((1, LN), F32))

    def fc2_fwd(i, _):
        at = rows_at(i * CH, CH)
        part3[at, :] = nt(hid[at, :], wc[...]).astype(BF)
        return 0

    def grad_full(full, left, right):
        for k in range(3):
            full[384 * k : 384 * k + 384, :] = tn(left[:, 384 * k : 384 * k + 384], right[...])

    def x_start(g, full):
        for zz in range(4):
            xs[g, zz] = full[rows_at((2 * zz + 1 - core) * BLK, BLK), :].astype(BF)
        cp = rcopy(xs.at[g], xr.at[g], x_s.at[g], x_r.at[g], sib)
        cp.start()
        pending.append(cp)

    def z_start(g, full):
        rcopy(xs.at[g], xr.at[g], x_s.at[g], x_r.at[g], sib).wait_recv()
        for d in (2, 1, 3):
            zz = zoff(d)
            zs[g, zz] = (
                full[rows_at((2 * zz + core) * BLK, BLK), :] + xr[g, zz].astype(F32)
            ).astype(BF)
            cp = rcopy(zs.at[g, zz], zr.at[g, d], z_s.at[g, d], z_r.at[g, d], zdev(zz))
            cp.start()
            pending.append(cp)

    def c_start(g, full):
        total = full[rows_at((2 * z + core) * BLK, BLK), :] + xr[g, z].astype(F32)
        for d in range(1, 4):
            rcopy(zs.at[g, 0], zr.at[g, d], z_s.at[g, d], z_r.at[g, d], zdev(zoff(d))).wait_recv()
            total = total + zr[g, d].astype(F32)
        cs[g] = total.astype(BF)
        cp = rcopy(cs.at[g], cr.at[g], c_s.at[g], c_r.at[g], octx)
        cp.start()
        pending.append(cp)

    def c_finish(g, ref):
        rcopy(cs.at[g], cr.at[g], c_s.at[g], c_r.at[g], octx).wait_recv()
        ref[...] = cs[g].astype(F32) + cr[g].astype(F32)

    grad_full(fullc, glow, hid)
    x_start(2, fullc)
    lax.fori_loop(0, 4, fc2_fwd, 0)

    g_mlp = rs_sum(1, part2, rr2)
    scaled = g_mlp * gain1
    normed_two = xh2[...]
    grad_y = glow[own, :].astype(F32)
    grad_after = grad_y + r2s[:, 0:1] * (
        scaled - mean_rows(scaled) - normed_two * mean_rows(scaled * normed_two)
    )
    gao[...] = grad_after
    g2[own, :] = grad_after.astype(BF)
    ag_start(1, g2)
    vecg[65:66, :] = jnp.sum(g_mlp * normed_two, axis=0, keepdims=True)
    vecg[67:68, :] = jnp.sum(g_mlp, axis=0, keepdims=True)
    vecg[68:69, :] = jnp.sum(grad_after, axis=0, keepdims=True)
    vecg[69:70, :] = jnp.sum(grad_y, axis=0, keepdims=True)

    z_start(2, fullc)
    grad_full(fullb, g1, gpb)
    x_start(1, fullb)

    ag_wait(1, g2)
    for j in range(8):
        rs_send(2, part3, rr3, lax.rem(t + j, 8))
    z_start(1, fullb)

    def grad_att(i, _):
        at = rows_at(i * 128, 128)
        low = nn(g2[at, :], wa[:, 0:256]).astype(BF)
        heads = nt(low, sela[...]).astype(BF)
        for h in range(2):
            gah[h, at, :] = heads[:, 128 * h : 128 * h + 128]
        return 0

    lax.fori_loop(0, 3, grad_att, 0)

    q_sums = []
    for h in range(2):

        def back(i, acc, h=h):
            at = rows_at(i * 128, 128)
            gh = gah[h, at, :]
            delta = jnp.sum(gh.astype(F32) * atth[h, at, :].astype(F32), axis=-1, keepdims=True)
            dso = (prob[h, at, 0:PAD] * (nt(gh, kvo[2 + h]) - delta)).astype(BF)
            dsx = (prob[h, at, PAD : 2 * PAD] * (nt(gh, kvx[2 + h]) - delta)).astype(BF)
            dsb[h, at, 0:PAD] = dso
            dsb[h, at, PAD : 2 * PAD] = dsx
            dq = (nn(dso, kvo[h]) + nn(dsx, kvx[h])) * SCALE
            dqb[at, 128 * h : 128 * h + 128] = dq.astype(BF)
            return acc + jnp.sum(dq, axis=0, keepdims=True)

        q_sums.append(lax.fori_loop(0, 3, back, jnp.zeros((1, 128), F32)))

    for h in range(2):
        for which, left, right in ((h, qh, dsb), (2 + h, gah, pbf)):
            grad = tn(left[h], right[h])
            if which < 2:
                grad = grad * SCALE
            dks[which] = grad[0:80, PAD : 2 * PAD].astype(BF)
            dkown[which] = grad[:, 0:PAD]
            cp = rcopy(dks.at[which], dkr.at[which], dk_s.at[which], dk_r.at[which], octx)
            cp.start()
            pending.append(cp)

    c_start(2, fullc)
    for k in range(3):
        fulla[384 * k : 384 * k + 384, 0:256] = tn(g2[:, 384 * k : 384 * k + 384], att[...])
    lay = (aft[...] + rs_sum(2, part3, rr3) + bias3) * mask_at(t * OWN, OWN)
    g3[own, :] = lay.astype(BF)

    for j in range(4):
        rcopy(dks.at[j], dkr.at[j], dk_s.at[j], dk_r.at[j], octx).wait_recv()
        totb[128 * j : 128 * j + 80, :] = (dkown[j, 0:80, :] + dkr[j].astype(F32)).astype(BF)
        totb[128 * j + 80 : 128 * j + 128, :] = jnp.zeros((48, PAD), BF)

    gs[...] = (nn(dqb[...], sel[0:256, :]) + tn(totb[...], sel[256:768, :])).astype(BF)

    def qkv_back(i, acc):
        ch = rs_chunk(i)
        at = rows_at(ch * CH, CH)
        grad = nt(gs[at, :], wa[:, 128:640])
        part4[at, :] = grad.astype(BF)
        for b in range(2):
            rs_send(3, part4, rr4, ch * 2 + b)
        normed, _inv = stats(tokp[at, :].astype(F32))
        return (
            acc[0] + jnp.sum(grad * normed, axis=0, keepdims=True),
            acc[1] + jnp.sum(grad, axis=0, keepdims=True),
        )

    zero_row = jnp.zeros((1, D), F32)
    gain_sum, bias_sum = lax.fori_loop(0, 4, qkv_back, (zero_row, zero_row))
    ag_start(2, g3)
    vecg[64:65, :] = gain_sum
    vecg[66:67, :] = bias_sum

    ones = jnp.full((16, PAD), 1.0, BF)
    v_sum = nt(ones, totb[256:512, :])
    smx[0] = jnp.zeros((16, 128), F32)
    for k in range(5):
        smx[0, k : k + 1, :] = fc1_sum[:, 128 * k : 128 * k + 128]
    smx[0, 5:6, :] = q_sums[0]
    smx[0, 6:7, :] = q_sums[1]
    smx[0, 7:8, :] = v_sum[0:1, 0:128]
    smx[0, 8:9, :] = v_sum[0:1, 128:256]
    cp = rcopy(smx.at[0], smx.at[1], sx_s, sx_r, sib)
    cp.start()
    pending.append(cp)

    for k in range(3):
        at = slice(384 * k, 384 * k + 384)
        qkv_grad = tn(attin[:, at], gs[...])
        fulla[at, 128:256] = fulla[at, 128:256] + qkv_grad[:, 0:128]
        fulla[at, 256:512] = qkv_grad[:, 128:384]
        fulla[at, 512:640] = qkv_grad[:, 384:512] + vecg[:, at].T
    x_start(0, fulla)
    rcopy(smx.at[0], smx.at[1], sx_s, sx_r, sib).wait_recv()
    smz[z] = smx[0] + smx[1]
    for d in range(1, 4):
        cp = rcopy(smz.at[z], smz.at[z], sz_s.at[d], sz_r.at[z], zdev(zoff(d)))
        cp.start()
        pending.append(cp)
    z_start(0, fulla)
    c_start(1, fullb)

    g_in = rs_sum(3, part4, rr4)
    normed_one, inv_one = stats(tokp[own, :].astype(F32))
    scaled = g_in * gain0
    grad_tok = gao[...] + inv_one * (
        scaled - mean_rows(scaled) - normed_one * mean_rows(scaled * normed_one)
    )
    g4[own, :] = grad_tok.astype(BF)
    ag_start(3, g4)

    for d in range(1, 4):
        j = zoff(d)
        rcopy(smz.at[j], smz.at[j], sz_s.at[d], sz_r.at[j], zdev(j)).wait_recv()
    smc[0] = smz[0] + smz[1] + smz[2] + smz[3]
    cp = rcopy(smc.at[0], smc.at[1], sc_s, sc_r, octx)
    cp.start()
    pending.append(cp)
    c_start(0, fulla)
    c_finish(2, gc_ref)
    c_finish(1, gb_ref)
    ag_wait(2, g3)
    out_ref[...] = g3[0:ROWS, :]
    c_finish(0, ga_ref)
    wide = jnp.concatenate([ga_ref[:, 512:640], jnp.zeros((112, 128), F32)], axis=0)
    vt[t] = wide.T[64:72, :]
    for d in range(1, 8):
        cp = rcopy(vt.at[t], vt.at[t], v_s.at[d], v_r.at[t], {"tp": tpd(d)})
        cp.start()
        pending.append(cp)
    rcopy(smc.at[0], smc.at[1], sc_s, sc_r, octx).wait_recv()
    small_ref[...] = smc[0] + smc[1]
    ag_wait(3, g4)

    def spread(i, _):
        at = rows_at(i * 16, 16)
        gtok_ref[at, :] = g4[at, :].astype(F32)
        return 0

    lax.fori_loop(0, ROWS // 16, spread, 0)
    for d in range(1, 8):
        j = tpd(d)
        rcopy(vt.at[j], vt.at[j], v_s.at[d], v_r.at[j], {"tp": j}).wait_recv()
    total = vt[0]
    for j in range(1, 8):
        total = total + vt[j]
    vec_ref[...] = total

    for k, (part, rr) in enumerate(((part1, rr1), (part2, rr2), (part3, rr3), (part4, rr4))):
        rs_done(k, part, rr)
    for cp in pending:
        cp.wait_send()


def per_device(
    tokens, image_count, ln_gain, vec_bias, w_qkv, qv_bias, w_out, w_fc1, fc1_bias, w_fc2, cotangent
):
    slots, rows, width = tokens.shape
    lanes = LN - 4 * BLK - 6
    wa = jnp.concatenate(
        [w_out.T, w_qkv[0], w_qkv[1], w_qkv[2], ln_gain.T, vec_bias.T, jnp.zeros((BLK, lanes), BF)],
        axis=1,
    )
    wb = jnp.pad(w_fc1, ((0, 0), (0, LN - FF_OWN)))
    wc = jnp.pad(w_fc2.T, ((0, 0), (0, LN - FF_OWN)))
    zeros = jnp.zeros((BLK,), BF)
    row0 = jnp.concatenate([zeros[:16], qv_bias[0], zeros, qv_bias[1], jnp.zeros((192,), BF)])
    row1 = jnp.pad(fc1_bias, (0, LN - FF_OWN))
    bias_rows = jnp.concatenate(
        [row0[None], row1[None], jnp.zeros((6, LN), BF)], axis=0
    ).astype(F32)

    vm = pltpu.VMEM
    dma = pltpu.SemaphoreType.DMA
    scratch = [
        vm((D, LN), BF), vm((D, LN), BF), vm((D, LN), BF),
        vm((PAD, D), BF), vm((PAD, D), BF), vm((PAD, D), BF),
        vm((2, PAD, 128), BF), vm((4, PAD, 128), BF), vm((4, PAD, 128), BF),
        vm((768, 512), BF), vm((256, 256), BF),
        vm((2, PAD, 2 * PAD), F32),
        vm((PAD, 256), BF), vm((2, PAD, 128), BF),
        vm((PAD, D), BF), vm((PAD, D), BF), vm((PAD, D), BF), vm((PAD, D), BF),
        vm((8, OWN, D), BF), vm((8, OWN, D), BF), vm((8, OWN, D), BF), vm((8, OWN, D), BF),
        vm((PAD, D), BF), vm((PAD, D), BF), vm((PAD, D), BF), vm((PAD, D), BF),
        vm((PAD, LN), F32), vm((PAD, LN), BF), vm((PAD, LN), BF),
        vm((OWN, D), F32), vm((OWN, D), F32), vm((OWN, 128), F32), vm((OWN, D), F32),
        vm((128, D), F32), vm((128, D), F32),
        vm((D, LN), F32), vm((D, LN), F32), vm((D, LN), F32),
        vm((3, 4, BLK, LN), BF), vm((3, 4, BLK, LN), BF),
        vm((3, 4, BLK, LN), BF), vm((3, 4, BLK, LN), BF),
        vm((3, BLK, LN), BF), vm((3, BLK, LN), BF),
        vm((512, PAD), BF), vm((4, 80, PAD), BF), vm((4, 80, PAD), BF), vm((4, 128, PAD), F32),
        vm((PAD, 256), BF), vm((2, PAD, 2 * PAD), BF), vm((2, PAD, 2 * PAD), BF),
        vm((2, PAD, 128), BF), vm((PAD, 512), BF),
        vm((2, 16, 128), F32), vm((4, 16, 128), F32), vm((2, 16, 128), F32), vm((8, 8, 256), F32),
        dma((3, 3)), dma((3, 3)), dma((3, 4)), dma((3, 4)),
        dma((4,)), dma((4,)), dma((4,)), dma((4,)),
        dma((4, 8)), dma((4, 8)), dma((4, 8)), dma((4, 8)),
        dma((3,)), dma((3,)), dma((3, 4)), dma((3, 4)), dma((3,)), dma((3,)),
        dma, dma, dma((4,)), dma((4,)), dma, dma,
        dma((8,)), dma((8,)),
    ]
    vspec = pl.BlockSpec(memory_space=pltpu.VMEM)
    out, gtok, ga, gb, gc, vec, small = pl.pallas_call(
        layer_kernel,
        out_shape=(
            jax.ShapeDtypeStruct((rows, width), BF),
            jax.ShapeDtypeStruct((rows, width), F32),
            jax.ShapeDtypeStruct((BLK, LN), F32),
            jax.ShapeDtypeStruct((BLK, LN), F32),
            jax.ShapeDtypeStruct((BLK, LN), F32),
            jax.ShapeDtypeStruct((8, 256), F32),
            jax.ShapeDtypeStruct((16, 128), F32),
        ),
        in_specs=[pl.BlockSpec(memory_space=pltpu.SMEM)] + [vspec] * 6,
        out_specs=tuple([vspec] * 7),
        scratch_shapes=scratch,
        compiler_params=pltpu.CompilerParams(
            collective_id=0, has_side_effects=True, vmem_limit_bytes=62 * 2**20
        ),
        name="encoder_layer",
    )(
        image_count,
        tokens.reshape(rows, width),
        cotangent.reshape(rows, width),
        wa,
        wb,
        wc,
        bias_rows,
    )
    gains = vec[0:2, 0:BLK]
    biases = vec[2:6, 0:BLK]
    grad_qkv = jnp.stack([ga[:, BLK * (k + 1) : BLK * (k + 2)] for k in range(3)])
    grad_out = ga[:, 0:BLK].T
    grad_qv = jnp.stack(
        [
            jnp.concatenate([small[5, :HD], small[6, :HD]]),
            jnp.concatenate([small[7, :HD], small[8, :HD]]),
        ]
    )
    fc1_bias_total = small[0:5].reshape(LN)[:FF_OWN]
    return (
        out.reshape(slots, rows, width),
        gtok.reshape(slots, rows, width),
        gains,
        biases,
        grad_qkv,
        grad_qv,
        grad_out,
        gb[:, :FF_OWN],
        fc1_bias_total,
        gc[:, :FF_OWN].T,
    )


def solution(mesh):
    placed = (
        P("shard", "ctx", None),
        P("shard"),
        P(None, "shard"),
        P(None, "shard"),
        P(None, "shard", "tp"),
        P(None, "tp"),
        P("tp", "shard"),
        P("shard", "tp"),
        P("tp"),
        P("tp", "shard"),
        P("shard", "ctx", None),
    )
    return jax.shard_map(
        per_device,
        mesh=mesh,
        in_specs=placed,
        out_specs=(
            P("shard", "ctx", None),
            P("shard", "ctx", None),
            P(None, "shard"),
            P(None, "shard"),
            P(None, "shard", "tp"),
            P(None, "tp"),
            P("tp", "shard"),
            P("shard", "tp"),
            P("tp"),
            P("tp", "shard"),
        ),
        check_vma=False,
    )
```

```python
import math

import jax
import jax.numpy as jnp
from jax import lax
from jax.experimental import pallas as pl
from jax.experimental.pallas import tpu as pltpu
from jax.sharding import PartitionSpec as P

HD = 72
IMG_TOK = 729
EPS = 1e-06
GELU_C = math.sqrt(2.0 / math.pi)
GELU_A = 0.044715
SCALE = HD ** (-0.5)

D = 1152
ROWS = 368
PAD = 384
OWN = 48
BLK = 144
LN = 640
FF_OWN = 538
CH = 96

MESH = pl.DeviceIdType.MESH
F32 = jnp.float32
BF = jnp.bfloat16


def nn(a, b):
    return jnp.dot(a, b, preferred_element_type=F32)


def nt(a, b):
    return lax.dot_general(a, b, (((1,), (1,)), ((), ())), preferred_element_type=F32)


def tn(a, b):
    return lax.dot_general(a, b, (((0,), (0,)), ((), ())), preferred_element_type=F32)


def mean_rows(x):
    return jnp.sum(x, axis=-1, keepdims=True) * (1.0 / D)


def rcopy(src, dst, send, recv, dev):
    return pltpu.make_async_remote_copy(
        src_ref=src,
        dst_ref=dst,
        send_sem=send,
        recv_sem=recv,
        device_id=dev,
        device_id_type=MESH,
    )


def rows_at(start, size, unit=16):
    if not isinstance(start, int):
        start = pl.multiple_of(start, unit)
    return pl.ds(start, size)


def layer_kernel(
    count,
    tok,
    cot,
    gain_in,
    vec_in,
    wqkv_in,
    qv_in,
    wout_in,
    fc1_in,
    fc1b_in,
    fc2_in,
    out_ref,
    gtok_ref,
    gain_out,
    vec_out,
    gqkv_out,
    gqv_out,
    gout_out,
    gfc1_out,
    gfc1b_out,
    gfc2_out,
    wa_in,
    wb_in,
    wc_in,
    bias_rows,
    vecs_in,
    ga_ref,
    wa,
    wb,
    wc,
    tokp,
    glow,
    attin,
    qh,
    kvo,
    kvx,
    sel,
    sela,
    prob,
    att,
    atth,
    part1,
    part2,
    part3,
    part4,
    rr1,
    rr2,
    rr3,
    rr4,
    g1,
    g2,
    g3,
    g4,
    gp0,
    hid,
    gpb,
    xh2,
    aft,
    r2s,
    gao,
    vrows,
    vecg,
    fulla,
    fullb,
    fullc,
    xs,
    xr,
    zs,
    zr,
    cs,
    cr,
    totb,
    dks,
    dkr,
    dkown,
    dqb,
    dsb,
    pbf,
    gah,
    gs,
    smx,
    smz,
    smc,
    vt,
    wz_s,
    wz_r,
    wc_s,
    wc_r,
    kv_s,
    kv_r,
    dk_s,
    dk_r,
    rs_s,
    rs_r,
    ag_s,
    ag_r,
    x_s,
    x_r,
    z_s,
    z_r,
    c_s,
    c_r,
    sx_s,
    sx_r,
    sz_s,
    sz_r,
    sc_s,
    sc_r,
    v_s,
    v_r,
):
    s = lax.axis_index("shard")
    c = lax.axis_index("ctx")
    t = lax.axis_index("tp")
    z = s // 2
    core = lax.rem(s, 2)
    sib = {"shard": z * 2 + 1 - core}
    octx = {"ctx": 1 - c}

    def zdev(zz):
        return {"shard": zz * 2 + core}

    def zoff(d):
        return lax.rem(z + d + 4, 4)

    def tpd(d):
        return lax.rem(t + d, 8)

    lo = t // 4
    ty = lax.rem(t, 4)

    def tpat(across, along):
        return lax.rem(lo + across, 2) * 4 + lax.rem(ty + along + 4, 4)

    def near_chunk(i):
        return lax.rem(lo + lax.div(i, 2), 2) * 2 + lax.rem(lax.div(ty, 2) + i, 2)

    pending = []

    bar = pltpu.get_barrier_semaphore()
    for d in range(1, 8):
        pl.semaphore_signal(bar, inc=1, device_id={"tp": tpd(d)}, device_id_type=MESH)
    for d in range(1, 4):
        pl.semaphore_signal(bar, inc=1, device_id=zdev(zoff(d)), device_id_type=MESH)
    pl.semaphore_signal(bar, inc=1, device_id=sib, device_id_type=MESH)
    pl.semaphore_signal(bar, inc=1, device_id=octx, device_id_type=MESH)

    def shifted(height, offset, lanes=LN):
        row = lax.broadcasted_iota(jnp.int32, (height, lanes), 0)
        lane = lax.broadcasted_iota(jnp.int32, (height, lanes), 1)
        return jnp.where(lane == row + offset, 1.0, 0.0).astype(BF)

    vecs_in[...] = jnp.zeros_like(vecs_in)
    vecs_in[0:2, :] = gain_in[...].astype(F32)
    vecs_in[2:6, :] = vec_in[...].astype(F32)
    packed = tn(wout_in[...], shifted(BLK, 0)) + tn(
        vecs_in[...].astype(BF), shifted(16, 4 * BLK)
    )
    for k in range(3):
        packed = packed + nn(wqkv_in[k], shifted(BLK, BLK * (k + 1)))
    wa_in[...] = packed.astype(BF)
    pl.semaphore_wait(bar, 12)

    groups = ((wa_in, wa), (wb_in, wb), (wc_in, wc))

    def block(ref, idx):
        return ref.at[rows_at(idx * BLK, BLK)]

    def w_start(g):
        src, full = groups[g]
        for d in (2, 1, 3):
            cp = rcopy(src, block(full, s), wz_s.at[g, d - 1], wz_r.at[g, d - 1], zdev(zoff(d)))
            cp.start()
            pending.append(cp)
        cp = rcopy(src, block(full, s), wc_s.at[g, 0], wc_r.at[g, 0], sib)
        cp.start()
        pending.append(cp)
        full[rows_at(s * BLK, BLK), :] = src[...]

    def w_forward(g):
        full = groups[g][1]
        for d in (1, 3, 2):
            got = block(full, zoff(-d) * 2 + core)
            rcopy(got, got, wz_s.at[g, d - 1], wz_r.at[g, d - 1], sib).wait_recv()
            cp = rcopy(got, got, wc_s.at[g, d], wc_r.at[g, d], sib)
            cp.start()
            pending.append(cp)

    def w_wait(g):
        full = groups[g][1]
        for d in range(4):
            got = block(full, zoff(-d) * 2 + 1 - core)
            rcopy(got, got, wc_s.at[g, d], wc_r.at[g, d], sib).wait_recv()

    w_start(0)
    for held, given in ((wb_in, fc1_in), (wc_in, fc2_in)):
        held[:, 512:LN] = jnp.zeros((BLK, LN - 512), BF)
        held[:, 0:FF_OWN] = given[...]
    vecs_in[8:10, :] = qv_in[...].astype(F32)
    qv_low = vecs_in[8:16, :].astype(BF)
    bias_rows[...] = jnp.zeros_like(bias_rows)
    bias_rows[1:2, 0:FF_OWN] = fc1b_in[...].astype(F32)
    bias_rows[0:1, :] = (
        nn(qv_low, shifted(BLK, 16))[0:1, :] + nn(qv_low, shifted(BLK, 16 + 2 * BLK))[1:2, :]
    )

    def rs_send(k, part, rr, j):
        @pl.when(j != t)
        def _():
            rcopy(
                part.at[rows_at(j * OWN, OWN)], rr.at[t], rs_s.at[k, j], rs_r.at[k, t], {"tp": j}
            ).start()

    def rs_sum(k, part, rr):
        total = part[rows_at(t * OWN, OWN), :].astype(F32)
        for d in range(1, 8):
            j = tpd(d)
            rcopy(rr.at[j], rr.at[j], rs_s.at[k, j], rs_r.at[k, j], {"tp": j}).wait_recv()
            total = total + rr[j].astype(F32)
        return total

    def rs_done(k, part, rr):
        for d in range(1, 8):
            j = tpd(d)
            rcopy(
                part.at[rows_at(j * OWN, OWN)], rr.at[t], rs_s.at[k, j], rs_r.at[k, t], {"tp": j}
            ).wait_send()

    across, opposite = tpat(1, 0), tpat(0, 2)

    def ag_send(k, buf, n, owner, dest):
        blk = buf.at[rows_at(owner * OWN, OWN)]
        cp = rcopy(blk, blk, ag_s.at[k, n], ag_r.at[k, owner], {"tp": dest})
        cp.start()
        pending.append(cp)

    def ag_recv(k, buf, owner):
        blk = buf.at[rows_at(owner * OWN, OWN)]
        rcopy(blk, blk, ag_s.at[k, 0], ag_r.at[k, owner], {"tp": across}).wait_recv()

    def ag_start(k, buf):
        for n, dest in enumerate((across, opposite, tpat(0, 1), tpat(0, -1))):
            ag_send(k, buf, n, t, dest)

    def ag_relay(k, buf):
        ag_recv(k, buf, across)
        ag_send(k, buf, 4, across, tpat(0, 1))
        ag_send(k, buf, 5, across, tpat(0, -1))
        ag_recv(k, buf, opposite)
        ag_send(k, buf, 6, opposite, across)

    def ag_wait_block(k, buf, j):
        @pl.when((j != t) & (j != across) & (j != opposite))
        def _():
            ag_recv(k, buf, j)

    def ag_wait(k, buf):
        for a, b in ((0, 1), (0, -1), (1, 1), (1, -1), (1, 2)):
            ag_recv(k, buf, tpat(a, b))

    row_i = lax.broadcasted_iota(jnp.int32, (128, 512), 0)
    lane_i = lax.broadcasted_iota(jnp.int32, (128, 512), 1)
    for j in range(6):
        hit = (lane_i == row_i + (16 + HD * j)) & (row_i < HD)
        sel[128 * j : 128 * j + 128, :] = jnp.where(hit, 1.0, 0.0).astype(BF)
    row_h = lax.broadcasted_iota(jnp.int32, (128, 256), 0)
    lane_h = lax.broadcasted_iota(jnp.int32, (128, 256), 1)
    for j in range(2):
        hit = (lane_h == row_h + HD * j) & (row_h < HD)
        sela[128 * j : 128 * j + 128, :] = jnp.where(hit, 1.0, 0.0).astype(BF)

    live = jnp.where(count[0] > 0, 1.0, 0.0)
    limit = IMG_TOK - c * ROWS

    def mask_at(start, size):
        pos = lax.broadcasted_iota(jnp.int32, (size, 1), 0) + start
        return jnp.where(pos < jnp.minimum(limit, ROWS), live, 0.0)

    def stats(x):
        centred = x - mean_rows(x)
        inv = lax.rsqrt(mean_rows(centred * centred) + EPS)
        return centred * inv, inv

    def prep(i, _):
        at = rows_at(i * 16, 16)
        tokp[at, :] = tok[at, :]
        glow[at, :] = (cot[at, :].astype(F32) * mask_at(i * 16, 16)).astype(BF)
        return 0

    lax.fori_loop(0, ROWS // 16, prep, 0)
    tokp[ROWS:PAD, :] = jnp.zeros((PAD - ROWS, D), BF)
    glow[ROWS:PAD, :] = jnp.zeros((PAD - ROWS, D), BF)
    vecg[...] = jnp.zeros_like(vecg)

    w_forward(0)
    w_start(1)
    w_start(2)
    w_wait(0)
    vrows[...] = wa[:, 512:640].astype(F32).T
    gain0 = vrows[64:65, :]
    gain1 = vrows[65:66, :]
    bias0 = vrows[66:67, :]
    bias1 = vrows[67:68, :]
    bias2 = vrows[68:69, :]
    bias3 = vrows[69:70, :]

    def norm_one(i, _):
        at = rows_at(i * 128, 128)
        normed, _inv = stats(tokp[at, :].astype(F32))
        attin[at, :] = (normed * gain0 + bias0).astype(BF)
        return 0

    lax.fori_loop(0, 3, norm_one, 0)

    low = (nn(attin[...], wa[:, 128:640]) + bias_rows[0:1, 0:512]).astype(BF)
    for j in (2, 3, 4, 5, 0, 1):
        head = nt(low, sel[128 * j : 128 * j + 128, :]).astype(BF)
        if j < 2:
            qh[j] = head
        else:
            kvo[j - 2] = head
            cp = rcopy(kvo.at[j - 2], kvx.at[j - 2], kv_s.at[j - 2], kv_r.at[j - 2], octx)
            cp.start()
            pending.append(cp)

    lane_k = lax.broadcasted_iota(jnp.int32, (128, PAD), 1)
    own_keys = jnp.minimum(limit, ROWS)
    other_keys = jnp.minimum(IMG_TOK - (1 - c) * ROWS, ROWS)

    def own_scores(i, _):
        at = rows_at(i * 128, 128)
        for h in range(2):
            sc = nt(qh[h, at, :], kvo[h]) * SCALE
            prob[h, at, 0:PAD] = jnp.where(lane_k < own_keys, sc, -1e30)
        return 0

    lax.fori_loop(0, 3, own_scores, 0)
    def kv_wait(j):
        rcopy(kvo.at[j], kvx.at[j], kv_s.at[j], kv_r.at[j], octx).wait_recv()

    kv_wait(0)
    kv_wait(1)

    def softmax(i, _):
        at = rows_at(i * 128, 128)
        for h in range(2):
            sc = nt(qh[h, at, :], kvx[h]) * SCALE
            sc = jnp.where(lane_k < other_keys, sc, -1e30)
            so = prob[h, at, 0:PAD]
            peak = jnp.maximum(
                jnp.max(sc, axis=-1, keepdims=True), jnp.max(so, axis=-1, keepdims=True)
            )
            eo = jnp.exp(so - peak)
            ex = jnp.exp(sc - peak)
            inv = 1.0 / (
                jnp.sum(eo, axis=-1, keepdims=True) + jnp.sum(ex, axis=-1, keepdims=True)
            )
            po = eo * inv
            px = ex * inv
            prob[h, at, 0:PAD] = po
            prob[h, at, PAD : 2 * PAD] = px
            pbf[h, at, 0:PAD] = po.astype(BF)
            pbf[h, at, PAD : 2 * PAD] = px.astype(BF)
        return 0

    lax.fori_loop(0, 3, softmax, 0)
    kv_wait(2)
    kv_wait(3)
    for h in range(2):
        low = nn(pbf[h, :, 0:PAD], kvo[2 + h]) + nn(pbf[h, :, PAD : 2 * PAD], kvx[2 + h])
        atth[h] = low.astype(BF)
    att[...] = (nn(atth[0], sela[0:128, :]) + nn(atth[1], sela[128:256, :])).astype(BF)

    def out_proj(i, _):
        ch = near_chunk(3 - i)
        at = rows_at(ch * CH, CH)
        part1[at, :] = nt(att[at, :], wa[:, 0:256]).astype(BF)
        for b in range(2):
            rs_send(0, part1, rr1, ch * 2 + b)
        return 0

    lax.fori_loop(0, 4, out_proj, 0)
    w_forward(1)
    w_forward(2)
    w_wait(1)
    w_wait(2)

    gp0[...] = nn(glow[...], wc[...])

    own = rows_at(t * OWN, OWN)
    after = tokp[own, :].astype(F32) + rs_sum(0, part1, rr1) + bias2
    aft[...] = after
    normed_two, inv_two = stats(after)
    xh2[...] = normed_two
    r2s[...] = jnp.broadcast_to(inv_two, (OWN, 128))
    g1[own, :] = (normed_two * gain1 + bias1).astype(BF)
    ag_start(0, g1)
    ag_relay(0, g1)

    def mlp(i, colsum):
        ch = near_chunk(i)
        at = rows_at(ch * CH, CH)
        for b in range(2):
            ag_wait_block(0, g1, ch * 2 + b)
        u = nn(g1[at, :], wb[...]) + bias_rows[1:2, :]
        uu = u * u
        tang = jnp.tanh(GELU_C * u * (1.0 + GELU_A * uu))
        hid[at, :] = (0.5 * u * (1.0 + tang)).astype(BF)
        slope = 0.5 * (1.0 + tang) + (0.5 * GELU_C) * u * (1.0 - tang * tang) * (
            1.0 + 3.0 * GELU_A * uu
        )
        gpre = gp0[at, :] * slope
        low = gpre.astype(BF)
        gpb[at, :] = low
        part2[at, :] = nt(low, wb[...]).astype(BF)
        for b in range(2):
            rs_send(1, part2, rr2, ch * 2 + b)
        return colsum + jnp.sum(gpre, axis=0, keepdims=True)

    fc1_sum = lax.fori_loop(0, 4, mlp, jnp.zeros((1, LN), F32))

    def grad_full(full, left, right):
        for k in range(3):
            full[384 * k : 384 * k + 384, :] = tn(left[:, 384 * k : 384 * k + 384], right[...])

    def x_start(g, full):
        for zz in range(4):
            xs[g, zz] = full[rows_at((2 * zz + 1 - core) * BLK, BLK), :].astype(BF)
        cp = rcopy(xs.at[g], xr.at[g], x_s.at[g], x_r.at[g], sib)
        cp.start()
        pending.append(cp)

    def z_start(g, full):
        rcopy(xs.at[g], xr.at[g], x_s.at[g], x_r.at[g], sib).wait_recv()
        for d in (2, 1, 3):
            zz = zoff(d)
            zs[g, zz] = (
                full[rows_at((2 * zz + core) * BLK, BLK), :] + xr[g, zz].astype(F32)
            ).astype(BF)
            cp = rcopy(zs.at[g, zz], zr.at[g, d], z_s.at[g, d], z_r.at[g, d], zdev(zz))
            cp.start()
            pending.append(cp)

    def c_start(g, full):
        total = full[rows_at((2 * z + core) * BLK, BLK), :] + xr[g, z].astype(F32)
        for d in range(1, 4):
            rcopy(zs.at[g, 0], zr.at[g, d], z_s.at[g, d], z_r.at[g, d], zdev(zoff(d))).wait_recv()
            total = total + zr[g, d].astype(F32)
        cs[g] = total.astype(BF)
        cp = rcopy(cs.at[g], cr.at[g], c_s.at[g], c_r.at[g], octx)
        cp.start()
        pending.append(cp)

    def c_finish(g):
        rcopy(cs.at[g], cr.at[g], c_s.at[g], c_r.at[g], octx).wait_recv()

    def cr_sum(g):
        return cs[g].astype(F32) + cr[g].astype(F32)

    grad_full(fullc, glow, hid)
    x_start(2, fullc)
    part3[...] = nt(hid[...], wc[...]).astype(BF)

    g_mlp = rs_sum(1, part2, rr2)
    scaled = g_mlp * gain1
    normed_two = xh2[...]
    grad_y = glow[own, :].astype(F32)
    grad_after = grad_y + r2s[:, 0:1] * (
        scaled - mean_rows(scaled) - normed_two * mean_rows(scaled * normed_two)
    )
    gao[...] = grad_after
    g2[own, :] = grad_after.astype(BF)
    ag_start(1, g2)
    vecg[65:66, :] = jnp.sum(g_mlp * normed_two, axis=0, keepdims=True)
    vecg[67:68, :] = jnp.sum(g_mlp, axis=0, keepdims=True)
    vecg[68:69, :] = jnp.sum(grad_after, axis=0, keepdims=True)
    vecg[69:70, :] = jnp.sum(grad_y, axis=0, keepdims=True)

    z_start(2, fullc)
    ag_relay(1, g2)
    grad_full(fullb, g1, gpb)
    x_start(1, fullb)

    ag_wait(1, g2)
    for j in range(8):
        rs_send(2, part3, rr3, lax.rem(t + j, 8))
    z_start(1, fullb)

    low = nn(g2[...], wa[:, 0:256]).astype(BF)
    for h in range(2):
        gah[h] = nt(low, sela[128 * h : 128 * h + 128, :]).astype(BF)

    q_sums = []
    for h in range(2):

        def back(i, acc, h=h):
            at = rows_at(i * 128, 128)
            gh = gah[h, at, :]
            delta = jnp.sum(gh.astype(F32) * atth[h, at, :].astype(F32), axis=-1, keepdims=True)
            dso = (prob[h, at, 0:PAD] * (nt(gh, kvo[2 + h]) - delta)).astype(BF)
            dsx = (prob[h, at, PAD : 2 * PAD] * (nt(gh, kvx[2 + h]) - delta)).astype(BF)
            dsb[h, at, 0:PAD] = dso
            dsb[h, at, PAD : 2 * PAD] = dsx
            dq = (nn(dso, kvo[h]) + nn(dsx, kvx[h])) * SCALE
            dqb[at, 128 * h : 128 * h + 128] = dq.astype(BF)
            return acc + jnp.sum(dq, axis=0, keepdims=True)

        q_sums.append(lax.fori_loop(0, 3, back, jnp.zeros((1, 128), F32)))

    for h in range(2):
        for which, left, right in ((h, qh, dsb), (2 + h, gah, pbf)):
            grad = tn(left[h], right[h])
            if which < 2:
                grad = grad * SCALE
            dks[which] = grad[0:80, PAD : 2 * PAD].astype(BF)
            dkown[which] = grad[:, 0:PAD]
            cp = rcopy(dks.at[which], dkr.at[which], dk_s.at[which], dk_r.at[which], octx)
            cp.start()
            pending.append(cp)

    c_start(2, fullc)
    c_start(1, fullb)
    for k in range(3):
        fulla[384 * k : 384 * k + 384, 0:256] = tn(g2[:, 384 * k : 384 * k + 384], att[...])
    lay = (aft[...] + rs_sum(2, part3, rr3) + bias3) * mask_at(t * OWN, OWN)
    g3[own, :] = lay.astype(BF)
    ag_start(2, g3)

    for j in range(4):
        rcopy(dks.at[j], dkr.at[j], dk_s.at[j], dk_r.at[j], octx).wait_recv()
        totb[128 * j : 128 * j + 80, :] = (dkown[j, 0:80, :] + dkr[j].astype(F32)).astype(BF)
        totb[128 * j + 80 : 128 * j + 128, :] = jnp.zeros((48, PAD), BF)

    gs[...] = (nn(dqb[...], sel[0:256, :]) + tn(totb[...], sel[256:768, :])).astype(BF)

    def qkv_back(i, acc):
        ch = near_chunk(3 - i)
        at = rows_at(ch * CH, CH)
        grad = nt(gs[at, :], wa[:, 128:640])
        part4[at, :] = grad.astype(BF)
        for b in range(2):
            rs_send(3, part4, rr4, ch * 2 + b)
        normed, _inv = stats(tokp[at, :].astype(F32))
        return (
            acc[0] + jnp.sum(grad * normed, axis=0, keepdims=True),
            acc[1] + jnp.sum(grad, axis=0, keepdims=True),
        )

    zero_row = jnp.zeros((1, D), F32)
    gain_sum, bias_sum = lax.fori_loop(0, 4, qkv_back, (zero_row, zero_row))
    ag_relay(2, g3)
    vecg[64:65, :] = gain_sum
    vecg[66:67, :] = bias_sum

    ones = jnp.full((16, PAD), 1.0, BF)
    v_sum = nt(ones, totb[256:512, :])
    smx[0] = jnp.zeros((16, 128), F32)
    for k in range(5):
        smx[0, k : k + 1, :] = fc1_sum[:, 128 * k : 128 * k + 128]
    smx[0, 5:6, :] = q_sums[0]
    smx[0, 6:7, :] = q_sums[1]
    smx[0, 7:8, :] = v_sum[0:1, 0:128]
    smx[0, 8:9, :] = v_sum[0:1, 128:256]
    cp = rcopy(smx.at[0], smx.at[1], sx_s, sx_r, sib)
    cp.start()
    pending.append(cp)

    for k in range(3):
        at = slice(384 * k, 384 * k + 384)
        qkv_grad = tn(attin[:, at], gs[...])
        fulla[at, 128:256] = fulla[at, 128:256] + qkv_grad[:, 0:128]
        fulla[at, 256:512] = qkv_grad[:, 128:384]
        fulla[at, 512:640] = qkv_grad[:, 384:512] + vecg[:, at].T
    x_start(0, fulla)
    rcopy(smx.at[0], smx.at[1], sx_s, sx_r, sib).wait_recv()
    smz[z] = smx[0] + smx[1]
    for d in range(1, 4):
        cp = rcopy(smz.at[z], smz.at[z], sz_s.at[d], sz_r.at[z], zdev(zoff(d)))
        cp.start()
        pending.append(cp)
    z_start(0, fulla)

    g_in = rs_sum(3, part4, rr4)
    normed_one, inv_one = stats(tokp[own, :].astype(F32))
    scaled = g_in * gain0
    grad_tok = gao[...] + inv_one * (
        scaled - mean_rows(scaled) - normed_one * mean_rows(scaled * normed_one)
    )
    g4[own, :] = grad_tok.astype(BF)
    ag_start(3, g4)
    c_finish(2)
    gfc2_out[...] = cr_sum(2)[:, 0:FF_OWN]
    c_finish(1)
    gfc1_out[...] = cr_sum(1)[:, 0:FF_OWN]
    ag_relay(3, g4)
    c_start(0, fulla)
    for d in range(1, 4):
        j = zoff(d)
        rcopy(smz.at[j], smz.at[j], sz_s.at[d], sz_r.at[j], zdev(j)).wait_recv()
    smc[0] = smz[0] + smz[1] + smz[2] + smz[3]
    cp = rcopy(smc.at[0], smc.at[1], sc_s, sc_r, octx)
    cp.start()
    pending.append(cp)
    ag_wait(2, g3)
    out_ref[...] = g3[0:ROWS, :]
    c_finish(0)
    ga_ref[...] = cr_sum(0)
    wide = jnp.concatenate([ga_ref[:, 512:640], jnp.zeros((112, 128), F32)], axis=0)
    vt[t] = wide.T[64:72, :]
    for d in range(1, 8):
        cp = rcopy(vt.at[t], vt.at[t], v_s.at[d], v_r.at[t], {"tp": tpd(d)})
        cp.start()
        pending.append(cp)
    for k in range(3):
        gqkv_out[k] = ga_ref[:, BLK * (k + 1) : BLK * (k + 2)]
    wide = jnp.concatenate([ga_ref[:, 0:256], jnp.zeros((112, 256), F32)], axis=0)
    gout_out[...] = wide.T[0:BLK, 0:BLK]
    rcopy(smc.at[0], smc.at[1], sc_s, sc_r, octx).wait_recv()
    small = smc[0] + smc[1]
    for k in range(4):
        gfc1b_out[0:1, 128 * k : 128 * k + 128] = small[k : k + 1, :]
    gfc1b_out[0:1, 512:FF_OWN] = small[4:5, 0 : FF_OWN - 512]
    for k in range(4):
        at = HD * (k % 2)
        gqv_out[k // 2 : k // 2 + 1, at : at + HD] = small[5 + k : 6 + k, 0:HD]
    ag_wait(3, g4)

    def spread(i, _):
        at = rows_at(i * 16, 16)
        gtok_ref[at, :] = g4[at, :].astype(F32)
        return 0

    lax.fori_loop(0, ROWS // 16, spread, 0)
    for d in range(1, 8):
        j = tpd(d)
        rcopy(vt.at[j], vt.at[j], v_s.at[d], v_r.at[j], {"tp": j}).wait_recv()
    total = vt[0]
    for j in range(1, 8):
        total = total + vt[j]
    gain_out[...] = total[0:2, 0:BLK]
    vec_out[...] = total[2:6, 0:BLK]

    for k, (part, rr) in enumerate(((part1, rr1), (part2, rr2), (part3, rr3), (part4, rr4))):
        rs_done(k, part, rr)
    for cp in pending:
        cp.wait_send()


def deliver(*refs):
    sems = refs[20]
    copies = [pltpu.make_async_copy(refs[i], refs[10 + i], sems.at[i]) for i in range(10)]
    for cp in copies:
        cp.start()
    for cp in copies:
        cp.wait()


def per_device(
    tokens, image_count, ln_gain, vec_bias, w_qkv, qv_bias, w_out, w_fc1, fc1_bias, w_fc2, cotangent
):
    slots, rows, width = tokens.shape
    vm = pltpu.VMEM
    dma = pltpu.SemaphoreType.DMA
    scratch = [
        vm((BLK, LN), BF), vm((BLK, LN), BF), vm((BLK, LN), BF),
        vm((8, LN), F32), vm((16, BLK), F32), vm((BLK, LN), F32),
        vm((D, LN), BF), vm((D, LN), BF), vm((D, LN), BF),
        vm((PAD, D), BF), vm((PAD, D), BF), vm((PAD, D), BF),
        vm((2, PAD, 128), BF), vm((4, PAD, 128), BF), vm((4, PAD, 128), BF),
        vm((768, 512), BF), vm((256, 256), BF),
        vm((2, PAD, 2 * PAD), F32),
        vm((PAD, 256), BF), vm((2, PAD, 128), BF),
        vm((PAD, D), BF), vm((PAD, D), BF), vm((PAD, D), BF), vm((PAD, D), BF),
        vm((8, OWN, D), BF), vm((8, OWN, D), BF), vm((8, OWN, D), BF), vm((8, OWN, D), BF),
        vm((PAD, D), BF), vm((PAD, D), BF), vm((PAD, D), BF), vm((PAD, D), BF),
        vm((PAD, LN), F32), vm((PAD, LN), BF), vm((PAD, LN), BF),
        vm((OWN, D), F32), vm((OWN, D), F32), vm((OWN, 128), F32), vm((OWN, D), F32),
        vm((128, D), F32), vm((128, D), F32),
        vm((D, LN), F32), vm((D, LN), F32), vm((D, LN), F32),
        vm((3, 4, BLK, LN), BF), vm((3, 4, BLK, LN), BF),
        vm((3, 4, BLK, LN), BF), vm((3, 4, BLK, LN), BF),
        vm((3, BLK, LN), BF), vm((3, BLK, LN), BF),
        vm((512, PAD), BF), vm((4, 80, PAD), BF), vm((4, 80, PAD), BF), vm((4, 128, PAD), F32),
        vm((PAD, 256), BF), vm((2, PAD, 2 * PAD), BF), vm((2, PAD, 2 * PAD), BF),
        vm((2, PAD, 128), BF), vm((PAD, 512), BF),
        vm((2, 16, 128), F32), vm((4, 16, 128), F32), vm((2, 16, 128), F32), vm((8, 8, 256), F32),
        dma((3, 3)), dma((3, 3)), dma((3, 4)), dma((3, 4)),
        dma((4,)), dma((4,)), dma((4,)), dma((4,)),
        dma((4, 8)), dma((4, 8)), dma((4, 8)), dma((4, 8)),
        dma((3,)), dma((3,)), dma((3, 4)), dma((3, 4)), dma((3,)), dma((3,)),
        dma, dma, dma((4,)), dma((4,)), dma, dma,
        dma((8,)), dma((8,)),
    ]
    vspec = pl.BlockSpec(memory_space=pltpu.VMEM)
    shapes = (
        jax.ShapeDtypeStruct((rows, width), BF),
        jax.ShapeDtypeStruct((rows, width), F32),
        jax.ShapeDtypeStruct((2, BLK), F32),
        jax.ShapeDtypeStruct((4, BLK), F32),
        jax.ShapeDtypeStruct((3, BLK, BLK), F32),
        jax.ShapeDtypeStruct((2, BLK), F32),
        jax.ShapeDtypeStruct((BLK, BLK), F32),
        jax.ShapeDtypeStruct((BLK, FF_OWN), F32),
        jax.ShapeDtypeStruct((1, FF_OWN), F32),
        jax.ShapeDtypeStruct((BLK, FF_OWN), F32),
    )
    results = pl.pallas_call(
        layer_kernel,
        out_shape=shapes,
        in_specs=[pl.BlockSpec(memory_space=pltpu.SMEM)] + [vspec] * 10,
        out_specs=tuple([vspec] * 10),
        scratch_shapes=scratch,
        compiler_params=pltpu.CompilerParams(
            collective_id=0, has_side_effects=True, vmem_limit_bytes=62 * 2**20
        ),
        name="encoder_layer",
    )(
        image_count,
        tokens.reshape(rows, width),
        cotangent.reshape(rows, width),
        ln_gain,
        vec_bias,
        w_qkv,
        qv_bias,
        w_out,
        w_fc1,
        fc1_bias.reshape(1, FF_OWN),
        w_fc2.T,
    )
    aspec = pl.BlockSpec(memory_space=pl.ANY)
    out, gtok, gains, biases, gqkv, gqv, gout, gfc1, gfc1b, gfc2 = pl.pallas_call(
        deliver,
        out_shape=shapes,
        in_specs=[aspec] * 10,
        out_specs=tuple([vspec] * 10),
        scratch_shapes=[pltpu.SemaphoreType.DMA((10,))],
        name="deliver",
    )(*results)
    return (
        out.reshape(slots, rows, width),
        gtok.reshape(slots, rows, width),
        gains,
        biases,
        gqkv,
        gqv,
        gout,
        gfc1,
        gfc1b.reshape(FF_OWN),
        gfc2.T,
    )


def solution(mesh):
    placed = (
        P("shard", "ctx", None),
        P("shard"),
        P(None, "shard"),
        P(None, "shard"),
        P(None, "shard", "tp"),
        P(None, "tp"),
        P("tp", "shard"),
        P("shard", "tp"),
        P("tp"),
        P("tp", "shard"),
        P("shard", "ctx", None),
    )
    return jax.shard_map(
        per_device,
        mesh=mesh,
        in_specs=placed,
        out_specs=(
            P("shard", "ctx", None),
            P("shard", "ctx", None),
            P(None, "shard"),
            P(None, "shard"),
            P(None, "shard", "tp"),
            P(None, "tp"),
            P("tp", "shard"),
            P("shard", "tp"),
            P("tp"),
            P("tp", "shard"),
        ),
        check_vma=False,
    )
```

```python
import math

import jax
import jax.numpy as jnp
from jax import lax
from jax.experimental import pallas as pl
from jax.experimental.pallas import tpu as pltpu
from jax.sharding import PartitionSpec as P

HD = 72
IMG_TOK = 729
EPS = 1e-06
GELU_C = math.sqrt(2.0 / math.pi)
GELU_A = 0.044715
SCALE = HD ** (-0.5)

D = 1152
ROWS = 368
PAD = 384
OWN = 48
BLK = 144
LN = 640
FF_OWN = 538
CH = 96

MESH = pl.DeviceIdType.MESH
F32 = jnp.float32
BF = jnp.bfloat16


def nn(a, b):
    return jnp.dot(a, b, preferred_element_type=F32)


def nt(a, b):
    return lax.dot_general(a, b, (((1,), (1,)), ((), ())), preferred_element_type=F32)


def tn(a, b):
    return lax.dot_general(a, b, (((0,), (0,)), ((), ())), preferred_element_type=F32)


def mean_rows(x):
    return jnp.sum(x, axis=-1, keepdims=True) * (1.0 / D)


def rcopy(src, dst, send, recv, dev):
    return pltpu.make_async_remote_copy(
        src_ref=src,
        dst_ref=dst,
        send_sem=send,
        recv_sem=recv,
        device_id=dev,
        device_id_type=MESH,
    )


def rows_at(start, size, unit=16):
    if not isinstance(start, int):
        start = pl.multiple_of(start, unit)
    return pl.ds(start, size)


def layer_kernel(
    count,
    tok,
    cot,
    gain_in,
    vec_in,
    wqkv_in,
    qv_in,
    wout_in,
    fc1_in,
    fc1b_in,
    fc2_in,
    out_ref,
    gtok_ref,
    gain_out,
    vec_out,
    gqkv_out,
    gqv_out,
    gout_out,
    gfc1_out,
    gfc1b_out,
    gfc2_out,
    wa_in,
    wb_in,
    wc_in,
    bias_rows,
    vecs_in,
    ga_ref,
    wa,
    wb,
    wc,
    tokp,
    glow,
    attin,
    qh,
    kvo,
    kvx,
    sel,
    sela,
    prob,
    att,
    atth,
    part1,
    part2,
    part3,
    part4,
    rr1,
    rr2,
    rr3,
    rr4,
    g1,
    g2,
    g3,
    g4,
    gp0,
    hid,
    gpb,
    xh2,
    aft,
    r2s,
    gao,
    vrows,
    vecg,
    fulla,
    fullb,
    fullc,
    xs,
    xr,
    zs,
    zr,
    cs,
    cr,
    totb,
    dks,
    dkr,
    dkown,
    dqb,
    dsb,
    pbf,
    gah,
    gs,
    smx,
    smz,
    smc,
    vt,
    wz_s,
    wz_r,
    wc_s,
    wc_r,
    kv_s,
    kv_r,
    dk_s,
    dk_r,
    rs_s,
    rs_r,
    ag_s,
    ag_r,
    x_s,
    x_r,
    z_s,
    z_r,
    c_s,
    c_r,
    sx_s,
    sx_r,
    sz_s,
    sz_r,
    sc_s,
    sc_r,
    v_s,
    v_r,
):
    s = lax.axis_index("shard")
    c = lax.axis_index("ctx")
    t = lax.axis_index("tp")
    z = s // 2
    core = lax.rem(s, 2)
    sib = {"shard": z * 2 + 1 - core}
    octx = {"ctx": 1 - c}

    def zdev(zz):
        return {"shard": zz * 2 + core}

    def zoff(d):
        return lax.rem(z + d + 4, 4)

    def tpd(d):
        return lax.rem(t + d, 8)

    lo = t // 4
    ty = lax.rem(t, 4)

    def tpat(across, along):
        return lax.rem(lo + across, 2) * 4 + lax.rem(ty + along + 4, 4)

    def near_chunk(i):
        return lax.rem(lo + lax.div(i, 2), 2) * 2 + lax.rem(lax.div(ty, 2) + i, 2)

    pending = []

    bar = pltpu.get_barrier_semaphore()
    for d in range(1, 8):
        pl.semaphore_signal(bar, inc=1, device_id={"tp": tpd(d)}, device_id_type=MESH)
    for d in range(1, 4):
        pl.semaphore_signal(bar, inc=1, device_id=zdev(zoff(d)), device_id_type=MESH)
    pl.semaphore_signal(bar, inc=1, device_id=sib, device_id_type=MESH)
    pl.semaphore_signal(bar, inc=1, device_id=octx, device_id_type=MESH)

    def shifted(height, offset, lanes=LN):
        row = lax.broadcasted_iota(jnp.int32, (height, lanes), 0)
        lane = lax.broadcasted_iota(jnp.int32, (height, lanes), 1)
        return jnp.where(lane == row + offset, 1.0, 0.0).astype(BF)

    vecs_in[...] = jnp.zeros_like(vecs_in)
    vecs_in[0:2, :] = gain_in[...].astype(F32)
    vecs_in[2:6, :] = vec_in[...].astype(F32)
    packed = tn(wout_in[...], shifted(BLK, 0)) + tn(
        vecs_in[...].astype(BF), shifted(16, 4 * BLK)
    )
    for k in range(3):
        packed = packed + nn(wqkv_in[k], shifted(BLK, BLK * (k + 1)))
    wa_in[...] = packed.astype(BF)
    pl.semaphore_wait(bar, 12)

    groups = ((wa_in, wa), (wb_in, wb), (wc_in, wc))

    def block(ref, idx):
        return ref.at[rows_at(idx * BLK, BLK)]

    def w_start(g):
        src, full = groups[g]
        for d in (2, 1, 3):
            cp = rcopy(src, block(full, s), wz_s.at[g, d - 1], wz_r.at[g, d - 1], zdev(zoff(d)))
            cp.start()
            pending.append(cp)
        cp = rcopy(src, block(full, s), wc_s.at[g, 0], wc_r.at[g, 0], sib)
        cp.start()
        pending.append(cp)
        full[rows_at(s * BLK, BLK), :] = src[...]

    def w_forward(g):
        full = groups[g][1]
        for d in (1, 3, 2):
            got = block(full, zoff(-d) * 2 + core)
            rcopy(got, got, wz_s.at[g, d - 1], wz_r.at[g, d - 1], sib).wait_recv()
            cp = rcopy(got, got, wc_s.at[g, d], wc_r.at[g, d], sib)
            cp.start()
            pending.append(cp)

    def w_wait(g):
        full = groups[g][1]
        for d in range(4):
            got = block(full, zoff(-d) * 2 + 1 - core)
            rcopy(got, got, wc_s.at[g, d], wc_r.at[g, d], sib).wait_recv()

    w_start(0)
    for held, given in ((wb_in, fc1_in), (wc_in, fc2_in)):
        held[:, 512:LN] = jnp.zeros((BLK, LN - 512), BF)
        held[:, 0:FF_OWN] = given[...]
    vecs_in[8:10, :] = qv_in[...].astype(F32)
    qv_low = vecs_in[8:16, :].astype(BF)
    bias_rows[...] = jnp.zeros_like(bias_rows)
    bias_rows[1:2, 0:FF_OWN] = fc1b_in[...].astype(F32).reshape(1, FF_OWN)
    bias_rows[0:1, :] = (
        nn(qv_low, shifted(BLK, 16))[0:1, :] + nn(qv_low, shifted(BLK, 16 + 2 * BLK))[1:2, :]
    )

    def rs_send(k, part, rr, j):
        @pl.when(j != t)
        def _():
            rcopy(
                part.at[rows_at(j * OWN, OWN)], rr.at[t], rs_s.at[k, j], rs_r.at[k, t], {"tp": j}
            ).start()

    def rs_sum(k, part, rr):
        total = part[rows_at(t * OWN, OWN), :].astype(F32)
        for d in range(1, 8):
            j = tpd(d)
            rcopy(rr.at[j], rr.at[j], rs_s.at[k, j], rs_r.at[k, j], {"tp": j}).wait_recv()
            total = total + rr[j].astype(F32)
        return total

    def rs_done(k, part, rr):
        for d in range(1, 8):
            j = tpd(d)
            rcopy(
                part.at[rows_at(j * OWN, OWN)], rr.at[t], rs_s.at[k, j], rs_r.at[k, t], {"tp": j}
            ).wait_send()

    across, opposite = tpat(1, 0), tpat(0, 2)

    def ag_send(k, buf, n, owner, dest):
        blk = buf.at[rows_at(owner * OWN, OWN)]
        cp = rcopy(blk, blk, ag_s.at[k, n], ag_r.at[k, owner], {"tp": dest})
        cp.start()
        pending.append(cp)

    def ag_recv(k, buf, owner):
        blk = buf.at[rows_at(owner * OWN, OWN)]
        rcopy(blk, blk, ag_s.at[k, 0], ag_r.at[k, owner], {"tp": across}).wait_recv()

    def ag_start(k, buf):
        for n, dest in enumerate((across, opposite, tpat(0, 1), tpat(0, -1))):
            ag_send(k, buf, n, t, dest)

    def ag_relay(k, buf):
        ag_recv(k, buf, across)
        ag_send(k, buf, 4, across, tpat(0, 1))
        ag_send(k, buf, 5, across, tpat(0, -1))
        ag_recv(k, buf, opposite)
        ag_send(k, buf, 6, opposite, across)

    def ag_wait_block(k, buf, j):
        @pl.when((j != t) & (j != across) & (j != opposite))
        def _():
            ag_recv(k, buf, j)

    def ag_wait(k, buf):
        for a, b in ((0, 1), (0, -1), (1, 1), (1, -1), (1, 2)):
            ag_recv(k, buf, tpat(a, b))

    row_i = lax.broadcasted_iota(jnp.int32, (128, 512), 0)
    lane_i = lax.broadcasted_iota(jnp.int32, (128, 512), 1)
    for j in range(6):
        hit = (lane_i == row_i + (16 + HD * j)) & (row_i < HD)
        sel[128 * j : 128 * j + 128, :] = jnp.where(hit, 1.0, 0.0).astype(BF)
    row_h = lax.broadcasted_iota(jnp.int32, (128, 256), 0)
    lane_h = lax.broadcasted_iota(jnp.int32, (128, 256), 1)
    for j in range(2):
        hit = (lane_h == row_h + HD * j) & (row_h < HD)
        sela[128 * j : 128 * j + 128, :] = jnp.where(hit, 1.0, 0.0).astype(BF)

    live = jnp.where(count[0] > 0, 1.0, 0.0)
    limit = IMG_TOK - c * ROWS

    def mask_at(start, size):
        pos = lax.broadcasted_iota(jnp.int32, (size, 1), 0) + start
        return jnp.where(pos < jnp.minimum(limit, ROWS), live, 0.0)

    def stats(x):
        centred = x - mean_rows(x)
        inv = lax.rsqrt(mean_rows(centred * centred) + EPS)
        return centred * inv, inv

    def prep(i, _):
        at = rows_at(i * 16, 16)
        tokp[at, :] = tok[at, :]
        glow[at, :] = (cot[at, :].astype(F32) * mask_at(i * 16, 16)).astype(BF)
        return 0

    lax.fori_loop(0, ROWS // 16, prep, 0)
    tokp[ROWS:PAD, :] = jnp.zeros((PAD - ROWS, D), BF)
    glow[ROWS:PAD, :] = jnp.zeros((PAD - ROWS, D), BF)
    vecg[...] = jnp.zeros_like(vecg)

    w_forward(0)
    w_start(1)
    w_start(2)
    w_wait(0)
    vrows[...] = wa[:, 512:640].astype(F32).T
    gain0 = vrows[64:65, :]
    gain1 = vrows[65:66, :]
    bias0 = vrows[66:67, :]
    bias1 = vrows[67:68, :]
    bias2 = vrows[68:69, :]
    bias3 = vrows[69:70, :]

    def norm_one(i, _):
        at = rows_at(i * 128, 128)
        normed, _inv = stats(tokp[at, :].astype(F32))
        attin[at, :] = (normed * gain0 + bias0).astype(BF)
        return 0

    lax.fori_loop(0, 3, norm_one, 0)

    low = (nn(attin[...], wa[:, 128:640]) + bias_rows[0:1, 0:512]).astype(BF)
    for j in (2, 3, 4, 5, 0, 1):
        head = nt(low, sel[128 * j : 128 * j + 128, :]).astype(BF)
        if j < 2:
            qh[j] = head
        else:
            kvo[j - 2] = head
            cp = rcopy(kvo.at[j - 2], kvx.at[j - 2], kv_s.at[j - 2], kv_r.at[j - 2], octx)
            cp.start()
            pending.append(cp)

    lane_k = lax.broadcasted_iota(jnp.int32, (128, PAD), 1)
    own_keys = jnp.minimum(limit, ROWS)
    other_keys = jnp.minimum(IMG_TOK - (1 - c) * ROWS, ROWS)

    def own_scores(i, _):
        at = rows_at(i * 128, 128)
        for h in range(2):
            sc = nt(qh[h, at, :], kvo[h]) * SCALE
            prob[h, at, 0:PAD] = jnp.where(lane_k < own_keys, sc, -1e30)
        return 0

    lax.fori_loop(0, 3, own_scores, 0)
    def kv_wait(j):
        rcopy(kvo.at[j], kvx.at[j], kv_s.at[j], kv_r.at[j], octx).wait_recv()

    kv_wait(0)
    kv_wait(1)

    def softmax(i, _):
        at = rows_at(i * 128, 128)
        for h in range(2):
            sc = nt(qh[h, at, :], kvx[h]) * SCALE
            sc = jnp.where(lane_k < other_keys, sc, -1e30)
            so = prob[h, at, 0:PAD]
            peak = jnp.maximum(
                jnp.max(sc, axis=-1, keepdims=True), jnp.max(so, axis=-1, keepdims=True)
            )
            eo = jnp.exp(so - peak)
            ex = jnp.exp(sc - peak)
            inv = 1.0 / (
                jnp.sum(eo, axis=-1, keepdims=True) + jnp.sum(ex, axis=-1, keepdims=True)
            )
            po = eo * inv
            px = ex * inv
            prob[h, at, 0:PAD] = po
            prob[h, at, PAD : 2 * PAD] = px
            pbf[h, at, 0:PAD] = po.astype(BF)
            pbf[h, at, PAD : 2 * PAD] = px.astype(BF)
        return 0

    lax.fori_loop(0, 3, softmax, 0)
    kv_wait(2)
    kv_wait(3)
    for h in range(2):
        low = nn(pbf[h, :, 0:PAD], kvo[2 + h]) + nn(pbf[h, :, PAD : 2 * PAD], kvx[2 + h])
        atth[h] = low.astype(BF)
    att[...] = (nn(atth[0], sela[0:128, :]) + nn(atth[1], sela[128:256, :])).astype(BF)

    def out_proj(i, _):
        ch = near_chunk(3 - i)
        at = rows_at(ch * CH, CH)
        part1[at, :] = nt(att[at, :], wa[:, 0:256]).astype(BF)
        for b in range(2):
            rs_send(0, part1, rr1, ch * 2 + b)
        return 0

    lax.fori_loop(0, 4, out_proj, 0)
    w_forward(1)
    w_forward(2)
    w_wait(1)
    w_wait(2)

    gp0[...] = nn(glow[...], wc[...])

    own = rows_at(t * OWN, OWN)
    after = tokp[own, :].astype(F32) + rs_sum(0, part1, rr1) + bias2
    aft[...] = after
    normed_two, inv_two = stats(after)
    xh2[...] = normed_two
    r2s[...] = jnp.broadcast_to(inv_two, (OWN, 128))
    g1[own, :] = (normed_two * gain1 + bias1).astype(BF)
    ag_start(0, g1)
    ag_relay(0, g1)

    def mlp(i, colsum):
        ch = near_chunk(i)
        at = rows_at(ch * CH, CH)
        for b in range(2):
            ag_wait_block(0, g1, ch * 2 + b)
        u = nn(g1[at, :], wb[...]) + bias_rows[1:2, :]
        uu = u * u
        tang = jnp.tanh(GELU_C * u * (1.0 + GELU_A * uu))
        hid[at, :] = (0.5 * u * (1.0 + tang)).astype(BF)
        slope = 0.5 * (1.0 + tang) + (0.5 * GELU_C) * u * (1.0 - tang * tang) * (
            1.0 + 3.0 * GELU_A * uu
        )
        gpre = gp0[at, :] * slope
        low = gpre.astype(BF)
        gpb[at, :] = low
        part2[at, :] = nt(low, wb[...]).astype(BF)
        for b in range(2):
            rs_send(1, part2, rr2, ch * 2 + b)
        return colsum + jnp.sum(gpre, axis=0, keepdims=True)

    fc1_sum = lax.fori_loop(0, 4, mlp, jnp.zeros((1, LN), F32))

    def grad_full(full, left, right):
        for k in range(3):
            full[384 * k : 384 * k + 384, :] = tn(left[:, 384 * k : 384 * k + 384], right[...])

    def x_start(g, full):
        for zz in range(4):
            xs[g, zz] = full[rows_at((2 * zz + 1 - core) * BLK, BLK), :].astype(BF)
        cp = rcopy(xs.at[g], xr.at[g], x_s.at[g], x_r.at[g], sib)
        cp.start()
        pending.append(cp)

    def z_start(g, full):
        rcopy(xs.at[g], xr.at[g], x_s.at[g], x_r.at[g], sib).wait_recv()
        for d in (2, 1, 3):
            zz = zoff(d)
            zs[g, zz] = (
                full[rows_at((2 * zz + core) * BLK, BLK), :] + xr[g, zz].astype(F32)
            ).astype(BF)
            cp = rcopy(zs.at[g, zz], zr.at[g, d], z_s.at[g, d], z_r.at[g, d], zdev(zz))
            cp.start()
            pending.append(cp)

    def c_start(g, full):
        total = full[rows_at((2 * z + core) * BLK, BLK), :] + xr[g, z].astype(F32)
        for d in range(1, 4):
            rcopy(zs.at[g, 0], zr.at[g, d], z_s.at[g, d], z_r.at[g, d], zdev(zoff(d))).wait_recv()
            total = total + zr[g, d].astype(F32)
        cs[g] = total.astype(BF)
        cp = rcopy(cs.at[g], cr.at[g], c_s.at[g], c_r.at[g], octx)
        cp.start()
        pending.append(cp)

    def c_finish(g):
        rcopy(cs.at[g], cr.at[g], c_s.at[g], c_r.at[g], octx).wait_recv()

    def cr_sum(g):
        return cs[g].astype(F32) + cr[g].astype(F32)

    part3[...] = nt(hid[...], wc[...]).astype(BF)
    for i in range(4):
        for b in range(2):
            rs_send(2, part3, rr3, near_chunk(3 - i) * 2 + b)
    grad_full(fullc, glow, hid)
    x_start(2, fullc)

    g_mlp = rs_sum(1, part2, rr2)
    scaled = g_mlp * gain1
    normed_two = xh2[...]
    grad_y = glow[own, :].astype(F32)
    grad_after = grad_y + r2s[:, 0:1] * (
        scaled - mean_rows(scaled) - normed_two * mean_rows(scaled * normed_two)
    )
    gao[...] = grad_after
    g2[own, :] = grad_after.astype(BF)
    ag_start(1, g2)
    vecg[65:66, :] = jnp.sum(g_mlp * normed_two, axis=0, keepdims=True)
    vecg[67:68, :] = jnp.sum(g_mlp, axis=0, keepdims=True)
    vecg[68:69, :] = jnp.sum(grad_after, axis=0, keepdims=True)
    vecg[69:70, :] = jnp.sum(grad_y, axis=0, keepdims=True)

    z_start(2, fullc)
    ag_relay(1, g2)
    grad_full(fullb, g1, gpb)
    x_start(1, fullb)

    ag_wait(1, g2)
    lay = (aft[...] + rs_sum(2, part3, rr3) + bias3) * mask_at(t * OWN, OWN)
    g3[own, :] = lay.astype(BF)
    ag_start(2, g3)

    low = nn(g2[...], wa[:, 0:256]).astype(BF)
    for h in range(2):
        gah[h] = nt(low, sela[128 * h : 128 * h + 128, :]).astype(BF)

    z_start(1, fullb)
    q_sums = []
    for h in range(2):

        def back(i, acc, h=h):
            at = rows_at(i * 128, 128)
            gh = gah[h, at, :]
            delta = jnp.sum(gh.astype(F32) * atth[h, at, :].astype(F32), axis=-1, keepdims=True)
            dso = (prob[h, at, 0:PAD] * (nt(gh, kvo[2 + h]) - delta)).astype(BF)
            dsx = (prob[h, at, PAD : 2 * PAD] * (nt(gh, kvx[2 + h]) - delta)).astype(BF)
            dsb[h, at, 0:PAD] = dso
            dsb[h, at, PAD : 2 * PAD] = dsx
            dq = (nn(dso, kvo[h]) + nn(dsx, kvx[h])) * SCALE
            dqb[at, 128 * h : 128 * h + 128] = dq.astype(BF)
            return acc + jnp.sum(dq, axis=0, keepdims=True)

        q_sums.append(lax.fori_loop(0, 3, back, jnp.zeros((1, 128), F32)))

    for h in range(2):
        for which, left, right in ((h, qh, dsb), (2 + h, gah, pbf)):
            grad = tn(left[h], right[h])
            if which < 2:
                grad = grad * SCALE
            dks[which] = grad[0:80, PAD : 2 * PAD].astype(BF)
            dkown[which] = grad[:, 0:PAD]
            cp = rcopy(dks.at[which], dkr.at[which], dk_s.at[which], dk_r.at[which], octx)
            cp.start()
            pending.append(cp)

    for k in range(3):
        fulla[384 * k : 384 * k + 384, 0:256] = tn(g2[:, 384 * k : 384 * k + 384], att[...])
    ag_relay(2, g3)

    for j in range(4):
        rcopy(dks.at[j], dkr.at[j], dk_s.at[j], dk_r.at[j], octx).wait_recv()
        totb[128 * j : 128 * j + 80, :] = (dkown[j, 0:80, :] + dkr[j].astype(F32)).astype(BF)
        totb[128 * j + 80 : 128 * j + 128, :] = jnp.zeros((48, PAD), BF)

    gs[...] = (nn(dqb[...], sel[0:256, :]) + tn(totb[...], sel[256:768, :])).astype(BF)

    def qkv_back(i, acc):
        ch = near_chunk(3 - i)
        at = rows_at(ch * CH, CH)
        grad = nt(gs[at, :], wa[:, 128:640])
        part4[at, :] = grad.astype(BF)
        for b in range(2):
            rs_send(3, part4, rr4, ch * 2 + b)
        normed, _inv = stats(tokp[at, :].astype(F32))
        return (
            acc[0] + jnp.sum(grad * normed, axis=0, keepdims=True),
            acc[1] + jnp.sum(grad, axis=0, keepdims=True),
        )

    zero_row = jnp.zeros((1, D), F32)
    gain_sum, bias_sum = lax.fori_loop(0, 4, qkv_back, (zero_row, zero_row))
    c_start(2, fullc)
    c_start(1, fullb)
    vecg[64:65, :] = gain_sum
    vecg[66:67, :] = bias_sum

    ones = jnp.full((16, PAD), 1.0, BF)
    v_sum = nt(ones, totb[256:512, :])
    smx[0] = jnp.zeros((16, 128), F32)
    for k in range(5):
        smx[0, k : k + 1, :] = fc1_sum[:, 128 * k : 128 * k + 128]
    smx[0, 5:6, :] = q_sums[0]
    smx[0, 6:7, :] = q_sums[1]
    smx[0, 7:8, :] = v_sum[0:1, 0:128]
    smx[0, 8:9, :] = v_sum[0:1, 128:256]
    cp = rcopy(smx.at[0], smx.at[1], sx_s, sx_r, sib)
    cp.start()
    pending.append(cp)

    for k in range(3):
        at = slice(384 * k, 384 * k + 384)
        qkv_grad = tn(attin[:, at], gs[...])
        fulla[at, 128:256] = fulla[at, 128:256] + qkv_grad[:, 0:128]
        fulla[at, 256:512] = qkv_grad[:, 128:384]
        fulla[at, 512:640] = qkv_grad[:, 384:512] + vecg[:, at].T
    x_start(0, fulla)
    rcopy(smx.at[0], smx.at[1], sx_s, sx_r, sib).wait_recv()
    smz[z] = smx[0] + smx[1]
    for d in range(1, 4):
        cp = rcopy(smz.at[z], smz.at[z], sz_s.at[d], sz_r.at[z], zdev(zoff(d)))
        cp.start()
        pending.append(cp)
    z_start(0, fulla)

    g_in = rs_sum(3, part4, rr4)
    normed_one, inv_one = stats(tokp[own, :].astype(F32))
    scaled = g_in * gain0
    grad_tok = gao[...] + inv_one * (
        scaled - mean_rows(scaled) - normed_one * mean_rows(scaled * normed_one)
    )
    g4[own, :] = grad_tok.astype(BF)
    ag_start(3, g4)
    c_finish(2)
    gfc2_out[...] = cr_sum(2)[:, 0:FF_OWN]
    c_finish(1)
    gfc1_out[...] = cr_sum(1)[:, 0:FF_OWN]
    ag_relay(3, g4)
    c_start(0, fulla)
    for d in range(1, 4):
        j = zoff(d)
        rcopy(smz.at[j], smz.at[j], sz_s.at[d], sz_r.at[j], zdev(j)).wait_recv()
    smc[0] = smz[0] + smz[1] + smz[2] + smz[3]
    cp = rcopy(smc.at[0], smc.at[1], sc_s, sc_r, octx)
    cp.start()
    pending.append(cp)
    ag_wait(2, g3)
    out_ref[...] = g3[0:ROWS, :]
    c_finish(0)
    ga_ref[...] = cr_sum(0)
    wide = jnp.concatenate([ga_ref[:, 512:640], jnp.zeros((112, 128), F32)], axis=0)
    vt[t] = wide.T[64:72, :]
    for d in range(1, 8):
        cp = rcopy(vt.at[t], vt.at[t], v_s.at[d], v_r.at[t], {"tp": tpd(d)})
        cp.start()
        pending.append(cp)
    for k in range(3):
        gqkv_out[k] = ga_ref[:, BLK * (k + 1) : BLK * (k + 2)]
    wide = jnp.concatenate([ga_ref[:, 0:256], jnp.zeros((112, 256), F32)], axis=0)
    gout_out[...] = wide.T[0:BLK, 0:BLK]
    rcopy(smc.at[0], smc.at[1], sc_s, sc_r, octx).wait_recv()
    small = smc[0] + smc[1]
    for k in range(4):
        gfc1b_out[0:1, 128 * k : 128 * k + 128] = small[k : k + 1, :]
    gfc1b_out[0:1, 512:FF_OWN] = small[4:5, 0 : FF_OWN - 512]
    for k in range(4):
        at = HD * (k % 2)
        gqv_out[k // 2 : k // 2 + 1, at : at + HD] = small[5 + k : 6 + k, 0:HD]
    ag_wait(3, g4)

    def spread(i, _):
        at = rows_at(i * 16, 16)
        gtok_ref[at, :] = g4[at, :].astype(F32)
        return 0

    lax.fori_loop(0, ROWS // 16, spread, 0)
    for d in range(1, 8):
        j = tpd(d)
        rcopy(vt.at[j], vt.at[j], v_s.at[d], v_r.at[j], {"tp": j}).wait_recv()
    total = vt[0]
    for j in range(1, 8):
        total = total + vt[j]
    gain_out[...] = total[0:2, 0:BLK]
    vec_out[...] = total[2:6, 0:BLK]

    for k, (part, rr) in enumerate(((part1, rr1), (part2, rr2), (part3, rr3), (part4, rr4))):
        rs_done(k, part, rr)
    for cp in pending:
        cp.wait_send()


def deliver(*refs):
    sems = refs[20]
    dests = list(refs[10:20])
    dests[8] = refs[21]
    copies = [pltpu.make_async_copy(refs[i], dests[i], sems.at[i]) for i in range(10)]
    for cp in copies:
        cp.start()
    for cp in copies:
        cp.wait()
    refs[18][...] = refs[21][...].reshape(FF_OWN)


def per_device(
    tokens, image_count, ln_gain, vec_bias, w_qkv, qv_bias, w_out, w_fc1, fc1_bias, w_fc2, cotangent
):
    slots, rows, width = tokens.shape
    vm = pltpu.VMEM
    dma = pltpu.SemaphoreType.DMA
    scratch = [
        vm((BLK, LN), BF), vm((BLK, LN), BF), vm((BLK, LN), BF),
        vm((8, LN), F32), vm((16, BLK), F32), vm((BLK, LN), F32),
        vm((D, LN), BF), vm((D, LN), BF), vm((D, LN), BF),
        vm((PAD, D), BF), vm((PAD, D), BF), vm((PAD, D), BF),
        vm((2, PAD, 128), BF), vm((4, PAD, 128), BF), vm((4, PAD, 128), BF),
        vm((768, 512), BF), vm((256, 256), BF),
        vm((2, PAD, 2 * PAD), F32),
        vm((PAD, 256), BF), vm((2, PAD, 128), BF),
        vm((PAD, D), BF), vm((PAD, D), BF), vm((PAD, D), BF), vm((PAD, D), BF),
        vm((8, OWN, D), BF), vm((8, OWN, D), BF), vm((8, OWN, D), BF), vm((8, OWN, D), BF),
        vm((PAD, D), BF), vm((PAD, D), BF), vm((PAD, D), BF), vm((PAD, D), BF),
        vm((PAD, LN), F32), vm((PAD, LN), BF), vm((PAD, LN), BF),
        vm((OWN, D), F32), vm((OWN, D), F32), vm((OWN, 128), F32), vm((OWN, D), F32),
        vm((128, D), F32), vm((128, D), F32),
        vm((D, LN), F32), vm((D, LN), F32), vm((D, LN), F32),
        vm((3, 4, BLK, LN), BF), vm((3, 4, BLK, LN), BF),
        vm((3, 4, BLK, LN), BF), vm((3, 4, BLK, LN), BF),
        vm((3, BLK, LN), BF), vm((3, BLK, LN), BF),
        vm((512, PAD), BF), vm((4, 80, PAD), BF), vm((4, 80, PAD), BF), vm((4, 128, PAD), F32),
        vm((PAD, 256), BF), vm((2, PAD, 2 * PAD), BF), vm((2, PAD, 2 * PAD), BF),
        vm((2, PAD, 128), BF), vm((PAD, 512), BF),
        vm((2, 16, 128), F32), vm((4, 16, 128), F32), vm((2, 16, 128), F32), vm((8, 8, 256), F32),
        dma((3, 3)), dma((3, 3)), dma((3, 4)), dma((3, 4)),
        dma((4,)), dma((4,)), dma((4,)), dma((4,)),
        dma((4, 8)), dma((4, 8)), dma((4, 8)), dma((4, 8)),
        dma((3,)), dma((3,)), dma((3, 4)), dma((3, 4)), dma((3,)), dma((3,)),
        dma, dma, dma((4,)), dma((4,)), dma, dma,
        dma((8,)), dma((8,)),
    ]
    vspec = pl.BlockSpec(memory_space=pltpu.VMEM)
    shapes = (
        jax.ShapeDtypeStruct((rows, width), BF),
        jax.ShapeDtypeStruct((rows, width), F32),
        jax.ShapeDtypeStruct((2, BLK), F32),
        jax.ShapeDtypeStruct((4, BLK), F32),
        jax.ShapeDtypeStruct((3, BLK, BLK), F32),
        jax.ShapeDtypeStruct((2, BLK), F32),
        jax.ShapeDtypeStruct((BLK, BLK), F32),
        jax.ShapeDtypeStruct((BLK, FF_OWN), F32),
        jax.ShapeDtypeStruct((1, FF_OWN), F32),
        jax.ShapeDtypeStruct((BLK, FF_OWN), F32),
    )
    results = pl.pallas_call(
        layer_kernel,
        out_shape=shapes,
        in_specs=[pl.BlockSpec(memory_space=pltpu.SMEM)] + [vspec] * 10,
        out_specs=tuple([vspec] * 10),
        scratch_shapes=scratch,
        compiler_params=pltpu.CompilerParams(
            collective_id=0, has_side_effects=True, vmem_limit_bytes=62 * 2**20
        ),
        name="encoder_layer",
    )(
        image_count,
        tokens.reshape(rows, width),
        cotangent.reshape(rows, width),
        ln_gain,
        vec_bias,
        w_qkv,
        qv_bias,
        w_out,
        w_fc1,
        fc1_bias,
        w_fc2.T,
    )
    aspec = pl.BlockSpec(memory_space=pl.ANY)
    out, gtok, gains, biases, gqkv, gqv, gout, gfc1, gfc1b, gfc2 = pl.pallas_call(
        deliver,
        out_shape=shapes[:8] + (jax.ShapeDtypeStruct((FF_OWN,), F32),) + shapes[9:],
        in_specs=[aspec] * 10,
        out_specs=tuple([vspec] * 10),
        scratch_shapes=[pltpu.SemaphoreType.DMA((10,)), pltpu.VMEM((1, FF_OWN), F32)],
        name="deliver",
    )(*results)
    return (
        out.reshape(slots, rows, width),
        gtok.reshape(slots, rows, width),
        gains,
        biases,
        gqkv,
        gqv,
        gout,
        gfc1,
        gfc1b,
        gfc2.T,
    )


def solution(mesh):
    placed = (
        P("shard", "ctx", None),
        P("shard"),
        P(None, "shard"),
        P(None, "shard"),
        P(None, "shard", "tp"),
        P(None, "tp"),
        P("tp", "shard"),
        P("shard", "tp"),
        P("tp"),
        P("tp", "shard"),
        P("shard", "ctx", None),
    )
    return jax.shard_map(
        per_device,
        mesh=mesh,
        in_specs=placed,
        out_specs=(
            P("shard", "ctx", None),
            P("shard", "ctx", None),
            P(None, "shard"),
            P(None, "shard"),
            P(None, "shard", "tp"),
            P(None, "tp"),
            P("tp", "shard"),
            P("shard", "tp"),
            P("tp"),
            P("tp", "shard"),
        ),
        check_vma=False,
    )
```

```python
import math

import jax
import jax.numpy as jnp
from jax import lax
from jax.experimental import pallas as pl
from jax.experimental.pallas import tpu as pltpu
from jax.sharding import PartitionSpec as P

HD = 72
IMG_TOK = 729
EPS = 1e-06
GELU_C = math.sqrt(2.0 / math.pi)
GELU_A = 0.044715
SCALE = HD ** (-0.5)

D = 1152
ROWS = 368
PAD = 384
OWN = 48
BLK = 144
LN = 640
FF_OWN = 538
CH = 96

MESH = pl.DeviceIdType.MESH
F32 = jnp.float32
BF = jnp.bfloat16


def nn(a, b):
    return jnp.dot(a, b, preferred_element_type=F32)


def nt(a, b):
    return lax.dot_general(a, b, (((1,), (1,)), ((), ())), preferred_element_type=F32)


def tn(a, b):
    return lax.dot_general(a, b, (((0,), (0,)), ((), ())), preferred_element_type=F32)


def mean_rows(x):
    return jnp.sum(x, axis=-1, keepdims=True) * (1.0 / D)


def rcopy(src, dst, send, recv, dev):
    return pltpu.make_async_remote_copy(
        src_ref=src,
        dst_ref=dst,
        send_sem=send,
        recv_sem=recv,
        device_id=dev,
        device_id_type=MESH,
    )


def rows_at(start, size, unit=16):
    if not isinstance(start, int):
        start = pl.multiple_of(start, unit)
    return pl.ds(start, size)


def layer_kernel(
    count,
    tok,
    cot,
    gain_in,
    vec_in,
    wqkv_in,
    qv_in,
    wout_in,
    fc1_in,
    fc1b_in,
    fc2_in,
    out_ref,
    gtok_ref,
    gain_out,
    vec_out,
    gqkv_out,
    gqv_out,
    gout_out,
    gfc1_out,
    gfc1b_out,
    gfc2_out,
    wa_in,
    wb_in,
    wc_in,
    bias_rows,
    vecs_in,
    ga_ref,
    wa,
    wb,
    wc,
    tokp,
    glow,
    attin,
    qh,
    kvo,
    kvx,
    sel,
    sela,
    prob,
    att,
    atth,
    part1,
    part2,
    part3,
    part4,
    rr1,
    rr2,
    rr3,
    rr4,
    g1,
    g2,
    g3,
    g4,
    gp0,
    hid,
    gpb,
    xh2,
    aft,
    r2s,
    gao,
    vrows,
    vecg,
    fulla,
    fullb,
    fullc,
    xs,
    xr,
    zs,
    zr,
    cs,
    cr,
    totb,
    dks,
    dkr,
    dkown,
    dqb,
    dsb,
    pbf,
    gah,
    gs,
    smx,
    smz,
    smc,
    vt,
    wz_s,
    wz_r,
    wc_s,
    wc_r,
    kv_s,
    kv_r,
    dk_s,
    dk_r,
    rs_s,
    rs_r,
    ag_s,
    ag_r,
    x_s,
    x_r,
    z_s,
    z_r,
    c_s,
    c_r,
    sx_s,
    sx_r,
    sz_s,
    sz_r,
    sc_s,
    sc_r,
    v_s,
    v_r,
):
    s = lax.axis_index("shard")
    c = lax.axis_index("ctx")
    t = lax.axis_index("tp")
    z = s // 2
    core = lax.rem(s, 2)
    sib = {"shard": z * 2 + 1 - core}
    octx = {"ctx": 1 - c}

    def zdev(zz):
        return {"shard": zz * 2 + core}

    def zoff(d):
        return lax.rem(z + d + 4, 4)

    def tpd(d):
        return lax.rem(t + d, 8)

    lo = t // 4
    ty = lax.rem(t, 4)

    def tpat(across, along):
        return lax.rem(lo + across, 2) * 4 + lax.rem(ty + along + 4, 4)

    def near_chunk(i):
        return lax.rem(lo + lax.div(i, 2), 2) * 2 + lax.rem(lax.div(ty, 2) + i, 2)

    pending = []

    bar = pltpu.get_barrier_semaphore()
    for d in range(1, 8):
        pl.semaphore_signal(bar, inc=1, device_id={"tp": tpd(d)}, device_id_type=MESH)
    for d in range(1, 4):
        pl.semaphore_signal(bar, inc=1, device_id=zdev(zoff(d)), device_id_type=MESH)
    pl.semaphore_signal(bar, inc=1, device_id=sib, device_id_type=MESH)
    pl.semaphore_signal(bar, inc=1, device_id=octx, device_id_type=MESH)

    def shifted(height, offset, lanes=LN):
        row = lax.broadcasted_iota(jnp.int32, (height, lanes), 0)
        lane = lax.broadcasted_iota(jnp.int32, (height, lanes), 1)
        return jnp.where(lane == row + offset, 1.0, 0.0).astype(BF)

    vecs_in[...] = jnp.zeros_like(vecs_in)
    vecs_in[0:2, :] = gain_in[...].astype(F32)
    vecs_in[2:6, :] = vec_in[...].astype(F32)
    packed = tn(wout_in[...], shifted(BLK, 0)) + tn(
        vecs_in[...].astype(BF), shifted(16, 4 * BLK)
    )
    for k in range(3):
        packed = packed + nn(wqkv_in[k], shifted(BLK, BLK * (k + 1)))
    wa_in[...] = packed.astype(BF)
    pl.semaphore_wait(bar, 12)

    groups = ((wa_in, wa), (wb_in, wb), (wc_in, wc))

    def block(ref, idx):
        return ref.at[rows_at(idx * BLK, BLK)]

    def w_start(g):
        src, full = groups[g]
        for d in (2, 1, 3):
            cp = rcopy(src, block(full, s), wz_s.at[g, d - 1], wz_r.at[g, d - 1], zdev(zoff(d)))
            cp.start()
            pending.append(cp)
        cp = rcopy(src, block(full, s), wc_s.at[g, 0], wc_r.at[g, 0], sib)
        cp.start()
        pending.append(cp)
        full[rows_at(s * BLK, BLK), :] = src[...]

    def w_forward(g):
        full = groups[g][1]
        for d in (1, 3, 2):
            got = block(full, zoff(-d) * 2 + core)
            rcopy(got, got, wz_s.at[g, d - 1], wz_r.at[g, d - 1], sib).wait_recv()
            cp = rcopy(got, got, wc_s.at[g, d], wc_r.at[g, d], sib)
            cp.start()
            pending.append(cp)

    def w_wait(g):
        full = groups[g][1]
        for d in range(4):
            got = block(full, zoff(-d) * 2 + 1 - core)
            rcopy(got, got, wc_s.at[g, d], wc_r.at[g, d], sib).wait_recv()

    w_start(0)
    for held, given in ((wb_in, fc1_in), (wc_in, fc2_in)):
        held[:, 512:LN] = jnp.zeros((BLK, LN - 512), BF)
        held[:, 0:FF_OWN] = given[...]
    vecs_in[8:10, :] = qv_in[...].astype(F32)
    qv_low = vecs_in[8:16, :].astype(BF)
    bias_rows[...] = jnp.zeros_like(bias_rows)
    bias_rows[1:2, 0:FF_OWN] = fc1b_in[...].astype(F32).reshape(1, FF_OWN)
    bias_rows[0:1, :] = (
        nn(qv_low, shifted(BLK, 16))[0:1, :] + nn(qv_low, shifted(BLK, 16 + 2 * BLK))[1:2, :]
    )

    across, opposite = tpat(1, 0), tpat(0, 2)

    def rs_copy(k, part, rr, j):
        slot = jnp.where(j // 4 == lo, ty, 4 + ty)
        return rcopy(
            part.at[rows_at(j * OWN, OWN)],
            rr.at[slot],
            rs_s.at[k, j],
            rs_r.at[k, slot],
            {"tp": lo * 4 + lax.rem(j, 4)},
        )

    def rs_send(k, part, rr, j):
        @pl.when(lax.rem(j, 4) != ty)
        def _():
            rs_copy(k, part, rr, j).start()

    def rs_recv(k, rr, slot):
        rcopy(rr.at[slot], rr.at[slot], rs_s.at[k, 0], rs_r.at[k, slot], {"tp": across}).wait_recv()

    def rs_cross(k, rr):
        return rcopy(
            rr.at[4 + ty], rr.at[ty], rs_s.at[k, across], rs_r.at[k, ty], {"tp": across}
        )

    def rs_relay(k, part, rr):
        total = part[rows_at(across * OWN, OWN), :].astype(F32)
        for d in range(1, 4):
            slot = 4 + lax.rem(ty + d, 4)
            rs_recv(k, rr, slot)
            total = total + rr[slot].astype(F32)
        rr[4 + ty] = total.astype(BF)
        rs_cross(k, rr).start()

    def rs_sum(k, part, rr):
        total = part[rows_at(t * OWN, OWN), :].astype(F32)
        for d in (1, 3, 2, 0):
            slot = lax.rem(ty + d, 4)
            rs_recv(k, rr, slot)
            total = total + rr[slot].astype(F32)
        return total

    def rs_done(k, part, rr):
        for d in range(1, 4):
            for a in range(2):
                rs_copy(k, part, rr, tpat(a, d)).wait_send()
        rs_cross(k, rr).wait_send()


    def ag_send(k, buf, n, owner, dest):
        blk = buf.at[rows_at(owner * OWN, OWN)]
        cp = rcopy(blk, blk, ag_s.at[k, n], ag_r.at[k, owner], {"tp": dest})
        cp.start()
        pending.append(cp)

    def ag_recv(k, buf, owner):
        blk = buf.at[rows_at(owner * OWN, OWN)]
        rcopy(blk, blk, ag_s.at[k, 0], ag_r.at[k, owner], {"tp": across}).wait_recv()

    def ag_start(k, buf):
        for n, dest in enumerate((across, opposite, tpat(0, 1), tpat(0, -1))):
            ag_send(k, buf, n, t, dest)

    def ag_relay(k, buf):
        ag_recv(k, buf, across)
        ag_send(k, buf, 4, across, tpat(0, 1))
        ag_send(k, buf, 5, across, tpat(0, -1))
        ag_recv(k, buf, opposite)
        ag_send(k, buf, 6, opposite, across)

    def ag_wait_block(k, buf, j):
        @pl.when((j != t) & (j != across) & (j != opposite))
        def _():
            ag_recv(k, buf, j)

    def ag_wait(k, buf):
        for a, b in ((0, 1), (0, -1), (1, 1), (1, -1), (1, 2)):
            ag_recv(k, buf, tpat(a, b))

    row_i = lax.broadcasted_iota(jnp.int32, (128, 512), 0)
    lane_i = lax.broadcasted_iota(jnp.int32, (128, 512), 1)
    for j in range(6):
        hit = (lane_i == row_i + (16 + HD * j)) & (row_i < HD)
        sel[128 * j : 128 * j + 128, :] = jnp.where(hit, 1.0, 0.0).astype(BF)
    row_h = lax.broadcasted_iota(jnp.int32, (128, 256), 0)
    lane_h = lax.broadcasted_iota(jnp.int32, (128, 256), 1)
    for j in range(2):
        hit = (lane_h == row_h + HD * j) & (row_h < HD)
        sela[128 * j : 128 * j + 128, :] = jnp.where(hit, 1.0, 0.0).astype(BF)

    live = jnp.where(count[0] > 0, 1.0, 0.0)
    limit = IMG_TOK - c * ROWS

    def mask_at(start, size):
        pos = lax.broadcasted_iota(jnp.int32, (size, 1), 0) + start
        return jnp.where(pos < jnp.minimum(limit, ROWS), live, 0.0)

    def stats(x):
        centred = x - mean_rows(x)
        inv = lax.rsqrt(mean_rows(centred * centred) + EPS)
        return centred * inv, inv

    def prep(i, _):
        at = rows_at(i * 16, 16)
        tokp[at, :] = tok[at, :]
        glow[at, :] = (cot[at, :].astype(F32) * mask_at(i * 16, 16)).astype(BF)
        return 0

    lax.fori_loop(0, ROWS // 16, prep, 0)
    tokp[ROWS:PAD, :] = jnp.zeros((PAD - ROWS, D), BF)
    glow[ROWS:PAD, :] = jnp.zeros((PAD - ROWS, D), BF)
    vecg[...] = jnp.zeros_like(vecg)

    w_forward(0)
    w_start(1)
    w_start(2)
    w_wait(0)
    vrows[...] = wa[:, 512:640].astype(F32).T
    gain0 = vrows[64:65, :]
    gain1 = vrows[65:66, :]
    bias0 = vrows[66:67, :]
    bias1 = vrows[67:68, :]
    bias2 = vrows[68:69, :]
    bias3 = vrows[69:70, :]

    def norm_one(i, _):
        at = rows_at(i * 128, 128)
        normed, _inv = stats(tokp[at, :].astype(F32))
        attin[at, :] = (normed * gain0 + bias0).astype(BF)
        return 0

    lax.fori_loop(0, 3, norm_one, 0)

    low = (nn(attin[...], wa[:, 128:640]) + bias_rows[0:1, 0:512]).astype(BF)
    for j in (2, 3, 4, 5, 0, 1):
        head = nt(low, sel[128 * j : 128 * j + 128, :]).astype(BF)
        if j < 2:
            qh[j] = head
        else:
            kvo[j - 2] = head
            cp = rcopy(kvo.at[j - 2], kvx.at[j - 2], kv_s.at[j - 2], kv_r.at[j - 2], octx)
            cp.start()
            pending.append(cp)

    lane_k = lax.broadcasted_iota(jnp.int32, (128, PAD), 1)
    own_keys = jnp.minimum(limit, ROWS)
    other_keys = jnp.minimum(IMG_TOK - (1 - c) * ROWS, ROWS)

    def own_scores(i, _):
        at = rows_at(i * 128, 128)
        for h in range(2):
            sc = nt(qh[h, at, :], kvo[h]) * SCALE
            prob[h, at, 0:PAD] = jnp.where(lane_k < own_keys, sc, -1e30)
        return 0

    lax.fori_loop(0, 3, own_scores, 0)
    def kv_wait(j):
        rcopy(kvo.at[j], kvx.at[j], kv_s.at[j], kv_r.at[j], octx).wait_recv()

    kv_wait(0)
    kv_wait(1)

    def softmax(i, _):
        at = rows_at(i * 128, 128)
        for h in range(2):
            sc = nt(qh[h, at, :], kvx[h]) * SCALE
            sc = jnp.where(lane_k < other_keys, sc, -1e30)
            so = prob[h, at, 0:PAD]
            peak = jnp.maximum(
                jnp.max(sc, axis=-1, keepdims=True), jnp.max(so, axis=-1, keepdims=True)
            )
            eo = jnp.exp(so - peak)
            ex = jnp.exp(sc - peak)
            inv = 1.0 / (
                jnp.sum(eo, axis=-1, keepdims=True) + jnp.sum(ex, axis=-1, keepdims=True)
            )
            po = eo * inv
            px = ex * inv
            prob[h, at, 0:PAD] = po
            prob[h, at, PAD : 2 * PAD] = px
            pbf[h, at, 0:PAD] = po.astype(BF)
            pbf[h, at, PAD : 2 * PAD] = px.astype(BF)
        return 0

    lax.fori_loop(0, 3, softmax, 0)
    kv_wait(2)
    kv_wait(3)
    for h in range(2):
        low = nn(pbf[h, :, 0:PAD], kvo[2 + h]) + nn(pbf[h, :, PAD : 2 * PAD], kvx[2 + h])
        atth[h] = low.astype(BF)
    att[...] = (nn(atth[0], sela[0:128, :]) + nn(atth[1], sela[128:256, :])).astype(BF)

    def out_proj(i, _):
        ch = near_chunk(3 - i)
        at = rows_at(ch * CH, CH)
        part1[at, :] = nt(att[at, :], wa[:, 0:256]).astype(BF)
        for b in range(2):
            rs_send(0, part1, rr1, ch * 2 + b)
        return 0

    lax.fori_loop(0, 4, out_proj, 0)
    w_forward(1)
    w_forward(2)
    rs_relay(0, part1, rr1)
    w_wait(1)
    w_wait(2)

    gp0[...] = nn(glow[...], wc[...])

    own = rows_at(t * OWN, OWN)
    after = tokp[own, :].astype(F32) + rs_sum(0, part1, rr1) + bias2
    aft[...] = after
    normed_two, inv_two = stats(after)
    xh2[...] = normed_two
    r2s[...] = jnp.broadcast_to(inv_two, (OWN, 128))
    g1[own, :] = (normed_two * gain1 + bias1).astype(BF)
    ag_start(0, g1)
    ag_relay(0, g1)

    def mlp(i, colsum):
        ch = near_chunk(i)
        at = rows_at(ch * CH, CH)
        for b in range(2):
            ag_wait_block(0, g1, ch * 2 + b)
        u = nn(g1[at, :], wb[...]) + bias_rows[1:2, :]
        uu = u * u
        tang = jnp.tanh(GELU_C * u * (1.0 + GELU_A * uu))
        hid[at, :] = (0.5 * u * (1.0 + tang)).astype(BF)
        slope = 0.5 * (1.0 + tang) + (0.5 * GELU_C) * u * (1.0 - tang * tang) * (
            1.0 + 3.0 * GELU_A * uu
        )
        gpre = gp0[at, :] * slope
        low = gpre.astype(BF)
        gpb[at, :] = low
        part2[at, :] = nt(low, wb[...]).astype(BF)
        for b in range(2):
            rs_send(1, part2, rr2, ch * 2 + b)
        return colsum + jnp.sum(gpre, axis=0, keepdims=True)

    fc1_sum = lax.fori_loop(0, 4, mlp, jnp.zeros((1, LN), F32))

    def grad_full(full, left, right):
        for k in range(3):
            full[384 * k : 384 * k + 384, :] = tn(left[:, 384 * k : 384 * k + 384], right[...])

    def x_start(g, full):
        for zz in range(4):
            xs[g, zz] = full[rows_at((2 * zz + 1 - core) * BLK, BLK), :].astype(BF)
        cp = rcopy(xs.at[g], xr.at[g], x_s.at[g], x_r.at[g], sib)
        cp.start()
        pending.append(cp)

    def z_start(g, full):
        rcopy(xs.at[g], xr.at[g], x_s.at[g], x_r.at[g], sib).wait_recv()
        for d in (2, 1, 3):
            zz = zoff(d)
            zs[g, zz] = (
                full[rows_at((2 * zz + core) * BLK, BLK), :] + xr[g, zz].astype(F32)
            ).astype(BF)
            cp = rcopy(zs.at[g, zz], zr.at[g, d], z_s.at[g, d], z_r.at[g, d], zdev(zz))
            cp.start()
            pending.append(cp)

    def c_start(g, full):
        total = full[rows_at((2 * z + core) * BLK, BLK), :] + xr[g, z].astype(F32)
        for d in range(1, 4):
            rcopy(zs.at[g, 0], zr.at[g, d], z_s.at[g, d], z_r.at[g, d], zdev(zoff(d))).wait_recv()
            total = total + zr[g, d].astype(F32)
        cs[g] = total.astype(BF)
        cp = rcopy(cs.at[g], cr.at[g], c_s.at[g], c_r.at[g], octx)
        cp.start()
        pending.append(cp)

    def c_finish(g):
        rcopy(cs.at[g], cr.at[g], c_s.at[g], c_r.at[g], octx).wait_recv()

    def cr_sum(g):
        return cs[g].astype(F32) + cr[g].astype(F32)

    part3[...] = nt(hid[...], wc[...]).astype(BF)
    for i in range(4):
        for b in range(2):
            rs_send(2, part3, rr3, near_chunk(3 - i) * 2 + b)
    rs_relay(1, part2, rr2)
    grad_full(fullc, glow, hid)
    x_start(2, fullc)

    g_mlp = rs_sum(1, part2, rr2)
    scaled = g_mlp * gain1
    normed_two = xh2[...]
    grad_y = glow[own, :].astype(F32)
    grad_after = grad_y + r2s[:, 0:1] * (
        scaled - mean_rows(scaled) - normed_two * mean_rows(scaled * normed_two)
    )
    gao[...] = grad_after
    g2[own, :] = grad_after.astype(BF)
    ag_start(1, g2)
    vecg[65:66, :] = jnp.sum(g_mlp * normed_two, axis=0, keepdims=True)
    vecg[67:68, :] = jnp.sum(g_mlp, axis=0, keepdims=True)
    vecg[68:69, :] = jnp.sum(grad_after, axis=0, keepdims=True)
    vecg[69:70, :] = jnp.sum(grad_y, axis=0, keepdims=True)

    z_start(2, fullc)
    rs_relay(2, part3, rr3)
    ag_relay(1, g2)
    grad_full(fullb, g1, gpb)
    x_start(1, fullb)

    z_start(1, fullb)
    ag_wait(1, g2)
    c_start(2, fullc)
    lay = (aft[...] + rs_sum(2, part3, rr3) + bias3) * mask_at(t * OWN, OWN)
    g3[own, :] = lay.astype(BF)
    ag_start(2, g3)

    low = nn(g2[...], wa[:, 0:256]).astype(BF)
    for h in range(2):
        gah[h] = nt(low, sela[128 * h : 128 * h + 128, :]).astype(BF)

    q_sums = []
    for h in range(2):

        def back(i, acc, h=h):
            at = rows_at(i * 128, 128)
            gh = gah[h, at, :]
            delta = jnp.sum(gh.astype(F32) * atth[h, at, :].astype(F32), axis=-1, keepdims=True)
            dso = (prob[h, at, 0:PAD] * (nt(gh, kvo[2 + h]) - delta)).astype(BF)
            dsx = (prob[h, at, PAD : 2 * PAD] * (nt(gh, kvx[2 + h]) - delta)).astype(BF)
            dsb[h, at, 0:PAD] = dso
            dsb[h, at, PAD : 2 * PAD] = dsx
            dq = (nn(dso, kvo[h]) + nn(dsx, kvx[h])) * SCALE
            dqb[at, 128 * h : 128 * h + 128] = dq.astype(BF)
            return acc + jnp.sum(dq, axis=0, keepdims=True)

        q_sums.append(lax.fori_loop(0, 3, back, jnp.zeros((1, 128), F32)))

    for h in range(2):
        for which, left, right in ((h, qh, dsb), (2 + h, gah, pbf)):
            grad = tn(left[h], right[h])
            if which < 2:
                grad = grad * SCALE
            dks[which] = grad[0:80, PAD : 2 * PAD].astype(BF)
            dkown[which] = grad[:, 0:PAD]
            cp = rcopy(dks.at[which], dkr.at[which], dk_s.at[which], dk_r.at[which], octx)
            cp.start()
            pending.append(cp)

    for k in range(3):
        fulla[384 * k : 384 * k + 384, 0:256] = tn(g2[:, 384 * k : 384 * k + 384], att[...])
    ag_relay(2, g3)

    for j in range(4):
        rcopy(dks.at[j], dkr.at[j], dk_s.at[j], dk_r.at[j], octx).wait_recv()
        totb[128 * j : 128 * j + 80, :] = (dkown[j, 0:80, :] + dkr[j].astype(F32)).astype(BF)
        totb[128 * j + 80 : 128 * j + 128, :] = jnp.zeros((48, PAD), BF)

    c_start(1, fullb)
    gs[...] = (nn(dqb[...], sel[0:256, :]) + tn(totb[...], sel[256:768, :])).astype(BF)

    def qkv_back(i, acc):
        ch = near_chunk(3 - i)
        at = rows_at(ch * CH, CH)
        grad = nt(gs[at, :], wa[:, 128:640])
        part4[at, :] = grad.astype(BF)
        for b in range(2):
            rs_send(3, part4, rr4, ch * 2 + b)
        normed, _inv = stats(tokp[at, :].astype(F32))
        return (
            acc[0] + jnp.sum(grad * normed, axis=0, keepdims=True),
            acc[1] + jnp.sum(grad, axis=0, keepdims=True),
        )

    zero_row = jnp.zeros((1, D), F32)
    gain_sum, bias_sum = lax.fori_loop(0, 4, qkv_back, (zero_row, zero_row))
    vecg[64:65, :] = gain_sum
    vecg[66:67, :] = bias_sum

    ones = jnp.full((16, PAD), 1.0, BF)
    v_sum = nt(ones, totb[256:512, :])
    smx[0] = jnp.zeros((16, 128), F32)
    for k in range(5):
        smx[0, k : k + 1, :] = fc1_sum[:, 128 * k : 128 * k + 128]
    smx[0, 5:6, :] = q_sums[0]
    smx[0, 6:7, :] = q_sums[1]
    smx[0, 7:8, :] = v_sum[0:1, 0:128]
    smx[0, 8:9, :] = v_sum[0:1, 128:256]
    cp = rcopy(smx.at[0], smx.at[1], sx_s, sx_r, sib)
    cp.start()
    pending.append(cp)

    for k in range(3):
        at = slice(384 * k, 384 * k + 384)
        qkv_grad = tn(attin[:, at], gs[...])
        fulla[at, 128:256] = fulla[at, 128:256] + qkv_grad[:, 0:128]
        fulla[at, 256:512] = qkv_grad[:, 128:384]
        fulla[at, 512:640] = qkv_grad[:, 384:512] + vecg[:, at].T
    x_start(0, fulla)
    rs_relay(3, part4, rr4)
    rcopy(smx.at[0], smx.at[1], sx_s, sx_r, sib).wait_recv()
    smz[z] = smx[0] + smx[1]
    for d in range(1, 4):
        cp = rcopy(smz.at[z], smz.at[z], sz_s.at[d], sz_r.at[z], zdev(zoff(d)))
        cp.start()
        pending.append(cp)
    z_start(0, fulla)

    g_in = rs_sum(3, part4, rr4)
    normed_one, inv_one = stats(tokp[own, :].astype(F32))
    scaled = g_in * gain0
    grad_tok = gao[...] + inv_one * (
        scaled - mean_rows(scaled) - normed_one * mean_rows(scaled * normed_one)
    )
    g4[own, :] = grad_tok.astype(BF)
    ag_start(3, g4)
    c_finish(2)
    gfc2_out[...] = cr_sum(2)[:, 0:FF_OWN]
    c_finish(1)
    gfc1_out[...] = cr_sum(1)[:, 0:FF_OWN]
    ag_relay(3, g4)
    c_start(0, fulla)
    for d in range(1, 4):
        j = zoff(d)
        rcopy(smz.at[j], smz.at[j], sz_s.at[d], sz_r.at[j], zdev(j)).wait_recv()
    smc[0] = smz[0] + smz[1] + smz[2] + smz[3]
    cp = rcopy(smc.at[0], smc.at[1], sc_s, sc_r, octx)
    cp.start()
    pending.append(cp)
    ag_wait(2, g3)
    out_ref[...] = g3[0:ROWS, :]
    c_finish(0)
    ga_ref[...] = cr_sum(0)
    wide = jnp.concatenate([ga_ref[:, 512:640], jnp.zeros((112, 128), F32)], axis=0)
    vt[t] = wide.T[64:72, :]
    for d in range(1, 8):
        cp = rcopy(vt.at[t], vt.at[t], v_s.at[d], v_r.at[t], {"tp": tpd(d)})
        cp.start()
        pending.append(cp)
    for k in range(3):
        gqkv_out[k] = ga_ref[:, BLK * (k + 1) : BLK * (k + 2)]
    wide = jnp.concatenate([ga_ref[:, 0:256], jnp.zeros((112, 256), F32)], axis=0)
    gout_out[...] = wide.T[0:BLK, 0:BLK]
    rcopy(smc.at[0], smc.at[1], sc_s, sc_r, octx).wait_recv()
    small = smc[0] + smc[1]
    for k in range(4):
        gfc1b_out[0:1, 128 * k : 128 * k + 128] = small[k : k + 1, :]
    gfc1b_out[0:1, 512:FF_OWN] = small[4:5, 0 : FF_OWN - 512]
    for k in range(4):
        at = HD * (k % 2)
        gqv_out[k // 2 : k // 2 + 1, at : at + HD] = small[5 + k : 6 + k, 0:HD]
    ag_wait(3, g4)

    def spread(i, _):
        at = rows_at(i * 16, 16)
        gtok_ref[at, :] = g4[at, :].astype(F32)
        return 0

    lax.fori_loop(0, ROWS // 16, spread, 0)
    for d in range(1, 8):
        j = tpd(d)
        rcopy(vt.at[j], vt.at[j], v_s.at[d], v_r.at[j], {"tp": j}).wait_recv()
    total = vt[0]
    for j in range(1, 8):
        total = total + vt[j]
    gain_out[...] = total[0:2, 0:BLK]
    vec_out[...] = total[2:6, 0:BLK]

    for k, (part, rr) in enumerate(((part1, rr1), (part2, rr2), (part3, rr3), (part4, rr4))):
        rs_done(k, part, rr)
    for cp in pending:
        cp.wait_send()


def deliver(*refs):
    sems = refs[20]
    dests = list(refs[10:20])
    dests[8] = refs[21]
    copies = [pltpu.make_async_copy(refs[i], dests[i], sems.at[i]) for i in range(10)]
    for cp in copies:
        cp.start()
    for cp in copies:
        cp.wait()
    refs[18][...] = refs[21][...].reshape(FF_OWN)


def per_device(
    tokens, image_count, ln_gain, vec_bias, w_qkv, qv_bias, w_out, w_fc1, fc1_bias, w_fc2, cotangent
):
    slots, rows, width = tokens.shape
    vm = pltpu.VMEM
    dma = pltpu.SemaphoreType.DMA
    scratch = [
        vm((BLK, LN), BF), vm((BLK, LN), BF), vm((BLK, LN), BF),
        vm((8, LN), F32), vm((16, BLK), F32), vm((BLK, LN), F32),
        vm((D, LN), BF), vm((D, LN), BF), vm((D, LN), BF),
        vm((PAD, D), BF), vm((PAD, D), BF), vm((PAD, D), BF),
        vm((2, PAD, 128), BF), vm((4, PAD, 128), BF), vm((4, PAD, 128), BF),
        vm((768, 512), BF), vm((256, 256), BF),
        vm((2, PAD, 2 * PAD), F32),
        vm((PAD, 256), BF), vm((2, PAD, 128), BF),
        vm((PAD, D), BF), vm((PAD, D), BF), vm((PAD, D), BF), vm((PAD, D), BF),
        vm((8, OWN, D), BF), vm((8, OWN, D), BF), vm((8, OWN, D), BF), vm((8, OWN, D), BF),
        vm((PAD, D), BF), vm((PAD, D), BF), vm((PAD, D), BF), vm((PAD, D), BF),
        vm((PAD, LN), F32), vm((PAD, LN), BF), vm((PAD, LN), BF),
        vm((OWN, D), F32), vm((OWN, D), F32), vm((OWN, 128), F32), vm((OWN, D), F32),
        vm((128, D), F32), vm((128, D), F32),
        vm((D, LN), F32), vm((D, LN), F32), vm((D, LN), F32),
        vm((3, 4, BLK, LN), BF), vm((3, 4, BLK, LN), BF),
        vm((3, 4, BLK, LN), BF), vm((3, 4, BLK, LN), BF),
        vm((3, BLK, LN), BF), vm((3, BLK, LN), BF),
        vm((512, PAD), BF), vm((4, 80, PAD), BF), vm((4, 80, PAD), BF), vm((4, 128, PAD), F32),
        vm((PAD, 256), BF), vm((2, PAD, 2 * PAD), BF), vm((2, PAD, 2 * PAD), BF),
        vm((2, PAD, 128), BF), vm((PAD, 512), BF),
        vm((2, 16, 128), F32), vm((4, 16, 128), F32), vm((2, 16, 128), F32), vm((8, 8, 256), F32),
        dma((3, 3)), dma((3, 3)), dma((3, 4)), dma((3, 4)),
        dma((4,)), dma((4,)), dma((4,)), dma((4,)),
        dma((4, 8)), dma((4, 8)), dma((4, 8)), dma((4, 8)),
        dma((3,)), dma((3,)), dma((3, 4)), dma((3, 4)), dma((3,)), dma((3,)),
        dma, dma, dma((4,)), dma((4,)), dma, dma,
        dma((8,)), dma((8,)),
    ]
    vspec = pl.BlockSpec(memory_space=pltpu.VMEM)
    shapes = (
        jax.ShapeDtypeStruct((rows, width), BF),
        jax.ShapeDtypeStruct((rows, width), F32),
        jax.ShapeDtypeStruct((2, BLK), F32),
        jax.ShapeDtypeStruct((4, BLK), F32),
        jax.ShapeDtypeStruct((3, BLK, BLK), F32),
        jax.ShapeDtypeStruct((2, BLK), F32),
        jax.ShapeDtypeStruct((BLK, BLK), F32),
        jax.ShapeDtypeStruct((BLK, FF_OWN), F32),
        jax.ShapeDtypeStruct((1, FF_OWN), F32),
        jax.ShapeDtypeStruct((BLK, FF_OWN), F32),
    )
    results = pl.pallas_call(
        layer_kernel,
        out_shape=shapes,
        in_specs=[pl.BlockSpec(memory_space=pltpu.SMEM)] + [vspec] * 10,
        out_specs=tuple([vspec] * 10),
        scratch_shapes=scratch,
        compiler_params=pltpu.CompilerParams(
            collective_id=0, has_side_effects=True, vmem_limit_bytes=62 * 2**20
        ),
        name="encoder_layer",
    )(
        image_count,
        tokens.reshape(rows, width),
        cotangent.reshape(rows, width),
        ln_gain,
        vec_bias,
        w_qkv,
        qv_bias,
        w_out,
        w_fc1,
        fc1_bias,
        w_fc2.T,
    )
    aspec = pl.BlockSpec(memory_space=pl.ANY)
    out, gtok, gains, biases, gqkv, gqv, gout, gfc1, gfc1b, gfc2 = pl.pallas_call(
        deliver,
        out_shape=shapes[:8] + (jax.ShapeDtypeStruct((FF_OWN,), F32),) + shapes[9:],
        in_specs=[aspec] * 10,
        out_specs=tuple([vspec] * 10),
        scratch_shapes=[pltpu.SemaphoreType.DMA((10,)), pltpu.VMEM((1, FF_OWN), F32)],
        name="deliver",
    )(*results)
    return (
        out.reshape(slots, rows, width),
        gtok.reshape(slots, rows, width),
        gains,
        biases,
        gqkv,
        gqv,
        gout,
        gfc1,
        gfc1b,
        gfc2.T,
    )


def solution(mesh):
    placed = (
        P("shard", "ctx", None),
        P("shard"),
        P(None, "shard"),
        P(None, "shard"),
        P(None, "shard", "tp"),
        P(None, "tp"),
        P("tp", "shard"),
        P("shard", "tp"),
        P("tp"),
        P("tp", "shard"),
        P("shard", "ctx", None),
    )
    return jax.shard_map(
        per_device,
        mesh=mesh,
        in_specs=placed,
        out_specs=(
            P("shard", "ctx", None),
            P("shard", "ctx", None),
            P(None, "shard"),
            P(None, "shard"),
            P(None, "shard", "tp"),
            P(None, "tp"),
            P("tp", "shard"),
            P("shard", "tp"),
            P("tp"),
            P("tp", "shard"),
        ),
        check_vma=False,
    )
```

```python
import math

import jax
import jax.numpy as jnp
from jax import lax
from jax.experimental import pallas as pl
from jax.experimental.pallas import tpu as pltpu
from jax.sharding import PartitionSpec as P

HD = 72
IMG_TOK = 729
EPS = 1e-06
GELU_C = math.sqrt(2.0 / math.pi)
GELU_A = 0.044715
SCALE = HD ** (-0.5)

D = 1152
ROWS = 368
PAD = 384
OWN = 48
BLK = 144
LN = 640
FF_OWN = 538
CH = 96

MESH = pl.DeviceIdType.MESH
F32 = jnp.float32
BF = jnp.bfloat16


def nn(a, b):
    return jnp.dot(a, b, preferred_element_type=F32)


def nt(a, b):
    return lax.dot_general(a, b, (((1,), (1,)), ((), ())), preferred_element_type=F32)


def tn(a, b):
    return lax.dot_general(a, b, (((0,), (0,)), ((), ())), preferred_element_type=F32)


def mean_rows(x):
    return jnp.sum(x, axis=-1, keepdims=True) * (1.0 / D)


def rcopy(src, dst, send, recv, dev):
    return pltpu.make_async_remote_copy(
        src_ref=src,
        dst_ref=dst,
        send_sem=send,
        recv_sem=recv,
        device_id=dev,
        device_id_type=MESH,
    )


def rows_at(start, size, unit=16):
    if not isinstance(start, int):
        start = pl.multiple_of(start, unit)
    return pl.ds(start, size)


def layer_kernel(
    count,
    tok,
    cot,
    gain_in,
    vec_in,
    wqkv_in,
    qv_in,
    wout_in,
    fc1_in,
    fc1b_in,
    fc2_in,
    out_ref,
    gtok_ref,
    gain_out,
    vec_out,
    gqkv_out,
    gqv_out,
    gout_out,
    gfc1_out,
    gfc1b_out,
    gfc2_out,
    wa_in,
    wb_in,
    wc_in,
    bias_rows,
    vecs_in,
    ga_ref,
    wa,
    wb,
    wc,
    tokp,
    glow,
    attin,
    qh,
    kvo,
    kvx,
    sel,
    sela,
    prob,
    att,
    atth,
    part1,
    part2,
    part3,
    part4,
    rr1,
    rr2,
    rr3,
    rr4,
    g1,
    g2,
    g3,
    g4,
    gp0,
    hid,
    gpb,
    xh2,
    aft,
    r2s,
    gao,
    vrows,
    vecg,
    fulla,
    fullb,
    fullc,
    xs,
    xr,
    zs,
    zr,
    cs,
    cr,
    totb,
    dks,
    dkr,
    dkown,
    dqb,
    dsb,
    pbf,
    gah,
    gs,
    smx,
    smz,
    smc,
    vt,
    wz_s,
    wz_r,
    wc_s,
    wc_r,
    kv_s,
    kv_r,
    dk_s,
    dk_r,
    rs_s,
    rs_r,
    ag_s,
    ag_r,
    x_s,
    x_r,
    z_s,
    z_r,
    c_s,
    c_r,
    sx_s,
    sx_r,
    sz_s,
    sz_r,
    sc_s,
    sc_r,
    v_s,
    v_r,
):
    s = lax.axis_index("shard")
    c = lax.axis_index("ctx")
    t = lax.axis_index("tp")
    z = s // 2
    core = lax.rem(s, 2)
    sib = {"shard": z * 2 + 1 - core}
    octx = {"ctx": 1 - c}

    def zdev(zz):
        return {"shard": zz * 2 + core}

    def zoff(d):
        return lax.rem(z + d + 4, 4)

    def tpd(d):
        return lax.rem(t + d, 8)

    lo = t // 4
    ty = lax.rem(t, 4)

    def tpat(across, along):
        return lax.rem(lo + across, 2) * 4 + lax.rem(ty + along + 4, 4)

    def near_chunk(i):
        return lax.rem(lo + lax.div(i, 2), 2) * 2 + lax.rem(lax.div(ty, 2) + i, 2)

    pending = []

    bar = pltpu.get_barrier_semaphore()
    for d in range(1, 8):
        pl.semaphore_signal(bar, inc=1, device_id={"tp": tpd(d)}, device_id_type=MESH)
    for d in range(1, 4):
        pl.semaphore_signal(bar, inc=1, device_id=zdev(zoff(d)), device_id_type=MESH)
    pl.semaphore_signal(bar, inc=1, device_id=sib, device_id_type=MESH)
    pl.semaphore_signal(bar, inc=1, device_id=octx, device_id_type=MESH)

    def shifted(height, offset, lanes=LN):
        row = lax.broadcasted_iota(jnp.int32, (height, lanes), 0)
        lane = lax.broadcasted_iota(jnp.int32, (height, lanes), 1)
        return jnp.where(lane == row + offset, 1.0, 0.0).astype(BF)

    vecs_in[...] = jnp.zeros_like(vecs_in)
    vecs_in[0:2, :] = gain_in[...].astype(F32)
    vecs_in[2:6, :] = vec_in[...].astype(F32)
    packed = tn(wout_in[...], shifted(BLK, 0)) + tn(
        vecs_in[...].astype(BF), shifted(16, 4 * BLK)
    )
    for k in range(3):
        packed = packed + nn(wqkv_in[k], shifted(BLK, BLK * (k + 1)))
    wa_in[...] = packed.astype(BF)
    pl.semaphore_wait(bar, 12)

    groups = ((wa_in, wa), (wb_in, wb), (wc_in, wc))

    def block(ref, idx):
        return ref.at[rows_at(idx * BLK, BLK)]

    def w_start(g):
        src, full = groups[g]
        for d in (2, 1, 3):
            cp = rcopy(src, block(full, s), wz_s.at[g, d - 1], wz_r.at[g, d - 1], zdev(zoff(d)))
            cp.start()
            pending.append(cp)
        cp = rcopy(src, block(full, s), wc_s.at[g, 0], wc_r.at[g, 0], sib)
        cp.start()
        pending.append(cp)
        full[rows_at(s * BLK, BLK), :] = src[...]

    def w_forward(g):
        full = groups[g][1]
        for d in (1, 3, 2):
            got = block(full, zoff(-d) * 2 + core)
            rcopy(got, got, wz_s.at[g, d - 1], wz_r.at[g, d - 1], sib).wait_recv()
            cp = rcopy(got, got, wc_s.at[g, d], wc_r.at[g, d], sib)
            cp.start()
            pending.append(cp)

    def w_wait(g):
        full = groups[g][1]
        for d in range(4):
            got = block(full, zoff(-d) * 2 + 1 - core)
            rcopy(got, got, wc_s.at[g, d], wc_r.at[g, d], sib).wait_recv()

    w_start(0)
    for held, given in ((wb_in, fc1_in), (wc_in, fc2_in)):
        held[:, 512:LN] = jnp.zeros((BLK, LN - 512), BF)
        held[:, 0:FF_OWN] = given[...]
    vecs_in[8:10, :] = qv_in[...].astype(F32)
    qv_low = vecs_in[8:16, :].astype(BF)
    bias_rows[...] = jnp.zeros_like(bias_rows)
    bias_rows[1:2, 0:FF_OWN] = fc1b_in[...].astype(F32).reshape(1, FF_OWN)
    bias_rows[0:1, :] = (
        nn(qv_low, shifted(BLK, 16))[0:1, :] + nn(qv_low, shifted(BLK, 16 + 2 * BLK))[1:2, :]
    )

    across, opposite = tpat(1, 0), tpat(0, 2)

    def rs_copy(k, part, rr, j):
        slot = jnp.where(j // 4 == lo, ty, 4 + ty)
        return rcopy(
            part.at[rows_at(j * OWN, OWN)],
            rr.at[slot],
            rs_s.at[k, j],
            rs_r.at[k, slot],
            {"tp": lo * 4 + lax.rem(j, 4)},
        )

    def rs_send(k, part, rr, j):
        @pl.when(lax.rem(j, 4) != ty)
        def _():
            rs_copy(k, part, rr, j).start()

    def rs_recv(k, rr, slot):
        rcopy(rr.at[slot], rr.at[slot], rs_s.at[k, 0], rs_r.at[k, slot], {"tp": across}).wait_recv()

    def rs_cross(k, rr):
        return rcopy(
            rr.at[4 + ty], rr.at[ty], rs_s.at[k, across], rs_r.at[k, ty], {"tp": across}
        )

    def rs_relay(k, part, rr):
        total = part[rows_at(across * OWN, OWN), :].astype(F32)
        for d in range(1, 4):
            slot = 4 + lax.rem(ty + d, 4)
            rs_recv(k, rr, slot)
            total = total + rr[slot].astype(F32)
        rr[4 + ty] = total.astype(BF)
        rs_cross(k, rr).start()

    def rs_sum(k, part, rr):
        total = part[rows_at(t * OWN, OWN), :].astype(F32)
        for d in (1, 3, 2, 0):
            slot = lax.rem(ty + d, 4)
            rs_recv(k, rr, slot)
            total = total + rr[slot].astype(F32)
        return total

    def rs_done(k, part, rr):
        for d in range(1, 4):
            for a in range(2):
                rs_copy(k, part, rr, tpat(a, d)).wait_send()
        rs_cross(k, rr).wait_send()


    def ag_send(k, buf, n, owner, dest):
        blk = buf.at[rows_at(owner * OWN, OWN)]
        cp = rcopy(blk, blk, ag_s.at[k, n], ag_r.at[k, owner], {"tp": dest})
        cp.start()
        pending.append(cp)

    def ag_recv(k, buf, owner):
        blk = buf.at[rows_at(owner * OWN, OWN)]
        rcopy(blk, blk, ag_s.at[k, 0], ag_r.at[k, owner], {"tp": across}).wait_recv()

    def ag_start(k, buf):
        for n, dest in enumerate((across, opposite, tpat(0, 1), tpat(0, -1))):
            ag_send(k, buf, n, t, dest)

    def ag_relay(k, buf):
        ag_recv(k, buf, across)
        ag_send(k, buf, 4, across, tpat(0, 1))
        ag_send(k, buf, 5, across, tpat(0, -1))
        ag_recv(k, buf, opposite)
        ag_send(k, buf, 6, opposite, across)

    def ag_wait_block(k, buf, j):
        @pl.when((j != t) & (j != across) & (j != opposite))
        def _():
            ag_recv(k, buf, j)

    def ag_wait(k, buf):
        for a, b in ((0, 1), (0, -1), (1, 1), (1, -1), (1, 2)):
            ag_recv(k, buf, tpat(a, b))

    row_i = lax.broadcasted_iota(jnp.int32, (128, 512), 0)
    lane_i = lax.broadcasted_iota(jnp.int32, (128, 512), 1)
    for j in range(6):
        hit = (lane_i == row_i + (16 + HD * j)) & (row_i < HD)
        sel[128 * j : 128 * j + 128, :] = jnp.where(hit, 1.0, 0.0).astype(BF)
    row_h = lax.broadcasted_iota(jnp.int32, (128, 256), 0)
    lane_h = lax.broadcasted_iota(jnp.int32, (128, 256), 1)
    for j in range(2):
        hit = (lane_h == row_h + HD * j) & (row_h < HD)
        sela[128 * j : 128 * j + 128, :] = jnp.where(hit, 1.0, 0.0).astype(BF)

    live = jnp.where(count[0] > 0, 1.0, 0.0)
    limit = IMG_TOK - c * ROWS

    def mask_at(start, size):
        pos = lax.broadcasted_iota(jnp.int32, (size, 1), 0) + start
        return jnp.where(pos < jnp.minimum(limit, ROWS), live, 0.0)

    def stats(x):
        centred = x - mean_rows(x)
        inv = lax.rsqrt(mean_rows(centred * centred) + EPS)
        return centred * inv, inv

    def prep(i, _):
        at = rows_at(i * 16, 16)
        tokp[at, :] = tok[at, :]
        glow[at, :] = (cot[at, :].astype(F32) * mask_at(i * 16, 16)).astype(BF)
        return 0

    lax.fori_loop(0, ROWS // 16, prep, 0)
    tokp[ROWS:PAD, :] = jnp.zeros((PAD - ROWS, D), BF)
    glow[ROWS:PAD, :] = jnp.zeros((PAD - ROWS, D), BF)
    vecg[...] = jnp.zeros_like(vecg)

    w_forward(0)
    w_start(1)
    w_start(2)
    w_wait(0)
    vrows[...] = wa[:, 512:640].astype(F32).T
    gain0 = vrows[64:65, :]
    gain1 = vrows[65:66, :]
    bias0 = vrows[66:67, :]
    bias1 = vrows[67:68, :]
    bias2 = vrows[68:69, :]
    bias3 = vrows[69:70, :]

    def norm_one(i, _):
        at = rows_at(i * 128, 128)
        normed, _inv = stats(tokp[at, :].astype(F32))
        attin[at, :] = (normed * gain0 + bias0).astype(BF)
        return 0

    lax.fori_loop(0, 3, norm_one, 0)

    low = (nn(attin[...], wa[:, 128:640]) + bias_rows[0:1, 0:512]).astype(BF)
    for j in (2, 3, 4, 5, 0, 1):
        head = nt(low, sel[128 * j : 128 * j + 128, :]).astype(BF)
        if j < 2:
            qh[j] = head
        else:
            kvo[j - 2] = head
            cp = rcopy(kvo.at[j - 2], kvx.at[j - 2], kv_s.at[j - 2], kv_r.at[j - 2], octx)
            cp.start()
            pending.append(cp)

    lane_k = lax.broadcasted_iota(jnp.int32, (128, PAD), 1)
    own_keys = jnp.minimum(limit, ROWS)
    other_keys = jnp.minimum(IMG_TOK - (1 - c) * ROWS, ROWS)

    def own_scores(i, _):
        at = rows_at(i * 128, 128)
        for h in range(2):
            sc = nt(qh[h, at, :], kvo[h]) * SCALE
            prob[h, at, 0:PAD] = jnp.where(lane_k < own_keys, sc, -1e30)
        return 0

    lax.fori_loop(0, 3, own_scores, 0)
    def kv_wait(j):
        rcopy(kvo.at[j], kvx.at[j], kv_s.at[j], kv_r.at[j], octx).wait_recv()

    kv_wait(0)
    kv_wait(1)

    def softmax(i, _):
        at = rows_at(i * 128, 128)
        for h in range(2):
            sc = nt(qh[h, at, :], kvx[h]) * SCALE
            sc = jnp.where(lane_k < other_keys, sc, -1e30)
            so = prob[h, at, 0:PAD]
            peak = jnp.maximum(
                jnp.max(sc, axis=-1, keepdims=True), jnp.max(so, axis=-1, keepdims=True)
            )
            eo = jnp.exp(so - peak)
            ex = jnp.exp(sc - peak)
            inv = 1.0 / (
                jnp.sum(eo, axis=-1, keepdims=True) + jnp.sum(ex, axis=-1, keepdims=True)
            )
            po = eo * inv
            px = ex * inv
            prob[h, at, 0:PAD] = po
            prob[h, at, PAD : 2 * PAD] = px
            pbf[h, at, 0:PAD] = po.astype(BF)
            pbf[h, at, PAD : 2 * PAD] = px.astype(BF)
        return 0

    lax.fori_loop(0, 3, softmax, 0)
    kv_wait(2)
    kv_wait(3)
    for h in range(2):
        low = nn(pbf[h, :, 0:PAD], kvo[2 + h]) + nn(pbf[h, :, PAD : 2 * PAD], kvx[2 + h])
        atth[h] = low.astype(BF)
    att[...] = (nn(atth[0], sela[0:128, :]) + nn(atth[1], sela[128:256, :])).astype(BF)

    def out_proj(i, _):
        ch = near_chunk(3 - i)
        at = rows_at(ch * CH, CH)
        part1[at, :] = nt(att[at, :], wa[:, 0:256]).astype(BF)
        for b in range(2):
            rs_send(0, part1, rr1, ch * 2 + b)
        return 0

    lax.fori_loop(0, 4, out_proj, 0)
    w_forward(1)
    w_forward(2)
    rs_relay(0, part1, rr1)
    w_wait(1)
    w_wait(2)

    gp0[...] = nn(glow[...], wc[...])

    own = rows_at(t * OWN, OWN)
    after = tokp[own, :].astype(F32) + rs_sum(0, part1, rr1) + bias2
    aft[...] = after
    normed_two, inv_two = stats(after)
    xh2[...] = normed_two
    r2s[...] = jnp.broadcast_to(inv_two, (OWN, 128))
    g1[own, :] = (normed_two * gain1 + bias1).astype(BF)
    ag_start(0, g1)
    ag_relay(0, g1)

    def mlp(i, colsum):
        ch = near_chunk(i)
        at = rows_at(ch * CH, CH)
        for b in range(2):
            ag_wait_block(0, g1, ch * 2 + b)
        u = nn(g1[at, :], wb[...]) + bias_rows[1:2, :]
        uu = u * u
        tang = jnp.tanh(GELU_C * u * (1.0 + GELU_A * uu))
        hid[at, :] = (0.5 * u * (1.0 + tang)).astype(BF)
        slope = 0.5 * (1.0 + tang) + (0.5 * GELU_C) * u * (1.0 - tang * tang) * (
            1.0 + 3.0 * GELU_A * uu
        )
        gpre = gp0[at, :] * slope
        low = gpre.astype(BF)
        gpb[at, :] = low
        part2[at, :] = nt(low, wb[...]).astype(BF)
        for b in range(2):
            rs_send(1, part2, rr2, ch * 2 + b)
        return colsum + jnp.sum(gpre, axis=0, keepdims=True)

    fc1_sum = lax.fori_loop(0, 4, mlp, jnp.zeros((1, LN), F32))

    def grad_full(full, left, right):
        for k in range(3):
            full[384 * k : 384 * k + 384, :] = tn(left[:, 384 * k : 384 * k + 384], right[...])

    def x_start(g, full):
        for zz in range(4):
            xs[g, zz] = full[rows_at((2 * zz + 1 - core) * BLK, BLK), :].astype(BF)
        cp = rcopy(xs.at[g], xr.at[g], x_s.at[g], x_r.at[g], sib)
        cp.start()
        pending.append(cp)

    def z_start(g, full):
        rcopy(xs.at[g], xr.at[g], x_s.at[g], x_r.at[g], sib).wait_recv()
        for d in (2, 1, 3):
            zz = zoff(d)
            zs[g, zz] = (
                full[rows_at((2 * zz + core) * BLK, BLK), :] + xr[g, zz].astype(F32)
            ).astype(BF)
            cp = rcopy(zs.at[g, zz], zr.at[g, d], z_s.at[g, d], z_r.at[g, d], zdev(zz))
            cp.start()
            pending.append(cp)

    def c_start(g, full):
        total = full[rows_at((2 * z + core) * BLK, BLK), :] + xr[g, z].astype(F32)
        for d in range(1, 4):
            rcopy(zs.at[g, 0], zr.at[g, d], z_s.at[g, d], z_r.at[g, d], zdev(zoff(d))).wait_recv()
            total = total + zr[g, d].astype(F32)
        cs[g] = total.astype(BF)
        cp = rcopy(cs.at[g], cr.at[g], c_s.at[g], c_r.at[g], octx)
        cp.start()
        pending.append(cp)

    def c_finish(g):
        rcopy(cs.at[g], cr.at[g], c_s.at[g], c_r.at[g], octx).wait_recv()

    def cr_sum(g):
        return cs[g].astype(F32) + cr[g].astype(F32)

    part3[...] = nt(hid[...], wc[...]).astype(BF)
    for i in range(4):
        for b in range(2):
            rs_send(2, part3, rr3, near_chunk(3 - i) * 2 + b)
    rs_relay(1, part2, rr2)
    grad_full(fullc, glow, hid)
    x_start(2, fullc)

    g_mlp = rs_sum(1, part2, rr2)
    scaled = g_mlp * gain1
    normed_two = xh2[...]
    grad_y = glow[own, :].astype(F32)
    grad_after = grad_y + r2s[:, 0:1] * (
        scaled - mean_rows(scaled) - normed_two * mean_rows(scaled * normed_two)
    )
    gao[...] = grad_after
    g2[own, :] = grad_after.astype(BF)
    ag_start(1, g2)
    vecg[65:66, :] = jnp.sum(g_mlp * normed_two, axis=0, keepdims=True)
    vecg[67:68, :] = jnp.sum(g_mlp, axis=0, keepdims=True)
    vecg[68:69, :] = jnp.sum(grad_after, axis=0, keepdims=True)
    vecg[69:70, :] = jnp.sum(grad_y, axis=0, keepdims=True)

    z_start(2, fullc)
    rs_relay(2, part3, rr3)
    ag_relay(1, g2)
    grad_full(fullb, g1, gpb)
    x_start(1, fullb)

    z_start(1, fullb)
    ag_wait(1, g2)
    c_start(2, fullc)
    lay = (aft[...] + rs_sum(2, part3, rr3) + bias3) * mask_at(t * OWN, OWN)
    g3[own, :] = lay.astype(BF)
    ag_start(2, g3)

    low = nn(g2[...], wa[:, 0:256]).astype(BF)
    for h in range(2):
        gah[h] = nt(low, sela[128 * h : 128 * h + 128, :]).astype(BF)

    q_sums = []
    for h in range(2):

        def back(i, acc, h=h):
            at = rows_at(i * 128, 128)
            gh = gah[h, at, :]
            delta = jnp.sum(gh.astype(F32) * atth[h, at, :].astype(F32), axis=-1, keepdims=True)
            dso = (prob[h, at, 0:PAD] * (nt(gh, kvo[2 + h]) - delta)).astype(BF)
            dsx = (prob[h, at, PAD : 2 * PAD] * (nt(gh, kvx[2 + h]) - delta)).astype(BF)
            dsb[h, at, 0:PAD] = dso
            dsb[h, at, PAD : 2 * PAD] = dsx
            dq = (nn(dso, kvo[h]) + nn(dsx, kvx[h])) * SCALE
            dqb[at, 128 * h : 128 * h + 128] = dq.astype(BF)
            return acc + jnp.sum(dq, axis=0, keepdims=True)

        q_sums.append(lax.fori_loop(0, 3, back, jnp.zeros((1, 128), F32)))

    for h in range(2):
        for which, left, right in ((h, qh, dsb), (2 + h, gah, pbf)):
            grad = tn(left[h], right[h])
            if which < 2:
                grad = grad * SCALE
            dks[which] = grad[0:80, PAD : 2 * PAD].astype(BF)
            dkown[which] = grad[:, 0:PAD]
            cp = rcopy(dks.at[which], dkr.at[which], dk_s.at[which], dk_r.at[which], octx)
            cp.start()
            pending.append(cp)

    for k in range(3):
        fulla[384 * k : 384 * k + 384, 0:256] = tn(g2[:, 384 * k : 384 * k + 384], att[...])
    ag_relay(2, g3)

    for j in range(4):
        rcopy(dks.at[j], dkr.at[j], dk_s.at[j], dk_r.at[j], octx).wait_recv()
        totb[128 * j : 128 * j + 80, :] = (dkown[j, 0:80, :] + dkr[j].astype(F32)).astype(BF)
        totb[128 * j + 80 : 128 * j + 128, :] = jnp.zeros((48, PAD), BF)

    gs[...] = (nn(dqb[...], sel[0:256, :]) + tn(totb[...], sel[256:768, :])).astype(BF)

    def qkv_back(i, acc):
        ch = near_chunk(3 - i)
        at = rows_at(ch * CH, CH)
        grad = nt(gs[at, :], wa[:, 128:640])
        part4[at, :] = grad.astype(BF)
        for b in range(2):
            rs_send(3, part4, rr4, ch * 2 + b)
        normed, _inv = stats(tokp[at, :].astype(F32))
        return (
            acc[0] + jnp.sum(grad * normed, axis=0, keepdims=True),
            acc[1] + jnp.sum(grad, axis=0, keepdims=True),
        )

    zero_row = jnp.zeros((1, D), F32)
    gain_sum, bias_sum = lax.fori_loop(0, 4, qkv_back, (zero_row, zero_row))
    vecg[64:65, :] = gain_sum
    vecg[66:67, :] = bias_sum

    ones = jnp.full((16, PAD), 1.0, BF)
    v_sum = nt(ones, totb[256:512, :])
    smx[0] = jnp.zeros((16, 128), F32)
    for k in range(5):
        smx[0, k : k + 1, :] = fc1_sum[:, 128 * k : 128 * k + 128]
    smx[0, 5:6, :] = q_sums[0]
    smx[0, 6:7, :] = q_sums[1]
    smx[0, 7:8, :] = v_sum[0:1, 0:128]
    smx[0, 8:9, :] = v_sum[0:1, 128:256]
    cp = rcopy(smx.at[0], smx.at[1], sx_s, sx_r, sib)
    cp.start()
    pending.append(cp)

    for k in range(3):
        at = slice(384 * k, 384 * k + 384)
        qkv_grad = tn(attin[:, at], gs[...])
        fulla[at, 128:256] = fulla[at, 128:256] + qkv_grad[:, 0:128]
        fulla[at, 256:512] = qkv_grad[:, 128:384]
        fulla[at, 512:640] = qkv_grad[:, 384:512] + vecg[:, at].T
    x_start(0, fulla)
    rs_relay(3, part4, rr4)
    rcopy(smx.at[0], smx.at[1], sx_s, sx_r, sib).wait_recv()
    smz[z] = smx[0] + smx[1]
    for d in range(1, 4):
        cp = rcopy(smz.at[z], smz.at[z], sz_s.at[d], sz_r.at[z], zdev(zoff(d)))
        cp.start()
        pending.append(cp)
    z_start(0, fulla)
    c_start(1, fullb)

    g_in = rs_sum(3, part4, rr4)
    normed_one, inv_one = stats(tokp[own, :].astype(F32))
    scaled = g_in * gain0
    grad_tok = gao[...] + inv_one * (
        scaled - mean_rows(scaled) - normed_one * mean_rows(scaled * normed_one)
    )
    g4[own, :] = grad_tok.astype(BF)
    ag_start(3, g4)
    c_finish(2)
    gfc2_out[...] = cr_sum(2)[:, 0:FF_OWN]
    c_finish(1)
    gfc1_out[...] = cr_sum(1)[:, 0:FF_OWN]
    ag_relay(3, g4)
    c_start(0, fulla)
    for d in range(1, 4):
        j = zoff(d)
        rcopy(smz.at[j], smz.at[j], sz_s.at[d], sz_r.at[j], zdev(j)).wait_recv()
    smc[0] = smz[0] + smz[1] + smz[2] + smz[3]
    cp = rcopy(smc.at[0], smc.at[1], sc_s, sc_r, octx)
    cp.start()
    pending.append(cp)
    ag_wait(2, g3)
    out_ref[...] = g3[0:ROWS, :]
    c_finish(0)
    ga_ref[...] = cr_sum(0)
    wide = jnp.concatenate([ga_ref[:, 512:640], jnp.zeros((112, 128), F32)], axis=0)
    vt[t] = wide.T[64:72, :]
    for d in range(1, 8):
        cp = rcopy(vt.at[t], vt.at[t], v_s.at[d], v_r.at[t], {"tp": tpd(d)})
        cp.start()
        pending.append(cp)
    for k in range(3):
        gqkv_out[k] = ga_ref[:, BLK * (k + 1) : BLK * (k + 2)]
    wide = jnp.concatenate([ga_ref[:, 0:256], jnp.zeros((112, 256), F32)], axis=0)
    gout_out[...] = wide.T[0:BLK, 0:BLK]
    rcopy(smc.at[0], smc.at[1], sc_s, sc_r, octx).wait_recv()
    small = smc[0] + smc[1]
    for k in range(4):
        gfc1b_out[0:1, 128 * k : 128 * k + 128] = small[k : k + 1, :]
    gfc1b_out[0:1, 512:FF_OWN] = small[4:5, 0 : FF_OWN - 512]
    for k in range(4):
        at = HD * (k % 2)
        gqv_out[k // 2 : k // 2 + 1, at : at + HD] = small[5 + k : 6 + k, 0:HD]
    ag_wait(3, g4)

    def spread(i, _):
        at = rows_at(i * 16, 16)
        gtok_ref[at, :] = g4[at, :].astype(F32)
        return 0

    lax.fori_loop(0, ROWS // 16, spread, 0)
    for d in range(1, 8):
        j = tpd(d)
        rcopy(vt.at[j], vt.at[j], v_s.at[d], v_r.at[j], {"tp": j}).wait_recv()
    total = vt[0]
    for j in range(1, 8):
        total = total + vt[j]
    gain_out[...] = total[0:2, 0:BLK]
    vec_out[...] = total[2:6, 0:BLK]

    for k, (part, rr) in enumerate(((part1, rr1), (part2, rr2), (part3, rr3), (part4, rr4))):
        rs_done(k, part, rr)
    for cp in pending:
        cp.wait_send()


def deliver(*refs):
    sems = refs[20]
    dests = list(refs[10:20])
    dests[8] = refs[21]
    copies = [pltpu.make_async_copy(refs[i], dests[i], sems.at[i]) for i in range(10)]
    for cp in copies:
        cp.start()
    for cp in copies:
        cp.wait()
    refs[18][...] = refs[21][...].reshape(FF_OWN)


def per_device(
    tokens, image_count, ln_gain, vec_bias, w_qkv, qv_bias, w_out, w_fc1, fc1_bias, w_fc2, cotangent
):
    slots, rows, width = tokens.shape
    vm = pltpu.VMEM
    dma = pltpu.SemaphoreType.DMA
    scratch = [
        vm((BLK, LN), BF), vm((BLK, LN), BF), vm((BLK, LN), BF),
        vm((8, LN), F32), vm((16, BLK), F32), vm((BLK, LN), F32),
        vm((D, LN), BF), vm((D, LN), BF), vm((D, LN), BF),
        vm((PAD, D), BF), vm((PAD, D), BF), vm((PAD, D), BF),
        vm((2, PAD, 128), BF), vm((4, PAD, 128), BF), vm((4, PAD, 128), BF),
        vm((768, 512), BF), vm((256, 256), BF),
        vm((2, PAD, 2 * PAD), F32),
        vm((PAD, 256), BF), vm((2, PAD, 128), BF),
        vm((PAD, D), BF), vm((PAD, D), BF), vm((PAD, D), BF), vm((PAD, D), BF),
        vm((8, OWN, D), BF), vm((8, OWN, D), BF), vm((8, OWN, D), BF), vm((8, OWN, D), BF),
        vm((PAD, D), BF), vm((PAD, D), BF), vm((PAD, D), BF), vm((PAD, D), BF),
        vm((PAD, LN), F32), vm((PAD, LN), BF), vm((PAD, LN), BF),
        vm((OWN, D), F32), vm((OWN, D), F32), vm((OWN, 128), F32), vm((OWN, D), F32),
        vm((128, D), F32), vm((128, D), F32),
        vm((D, LN), F32), vm((D, LN), F32), vm((D, LN), F32),
        vm((3, 4, BLK, LN), BF), vm((3, 4, BLK, LN), BF),
        vm((3, 4, BLK, LN), BF), vm((3, 4, BLK, LN), BF),
        vm((3, BLK, LN), BF), vm((3, BLK, LN), BF),
        vm((512, PAD), BF), vm((4, 80, PAD), BF), vm((4, 80, PAD), BF), vm((4, 128, PAD), F32),
        vm((PAD, 256), BF), vm((2, PAD, 2 * PAD), BF), vm((2, PAD, 2 * PAD), BF),
        vm((2, PAD, 128), BF), vm((PAD, 512), BF),
        vm((2, 16, 128), F32), vm((4, 16, 128), F32), vm((2, 16, 128), F32), vm((8, 8, 256), F32),
        dma((3, 3)), dma((3, 3)), dma((3, 4)), dma((3, 4)),
        dma((4,)), dma((4,)), dma((4,)), dma((4,)),
        dma((4, 8)), dma((4, 8)), dma((4, 8)), dma((4, 8)),
        dma((3,)), dma((3,)), dma((3, 4)), dma((3, 4)), dma((3,)), dma((3,)),
        dma, dma, dma((4,)), dma((4,)), dma, dma,
        dma((8,)), dma((8,)),
    ]
    vspec = pl.BlockSpec(memory_space=pltpu.VMEM)
    shapes = (
        jax.ShapeDtypeStruct((rows, width), BF),
        jax.ShapeDtypeStruct((rows, width), F32),
        jax.ShapeDtypeStruct((2, BLK), F32),
        jax.ShapeDtypeStruct((4, BLK), F32),
        jax.ShapeDtypeStruct((3, BLK, BLK), F32),
        jax.ShapeDtypeStruct((2, BLK), F32),
        jax.ShapeDtypeStruct((BLK, BLK), F32),
        jax.ShapeDtypeStruct((BLK, FF_OWN), F32),
        jax.ShapeDtypeStruct((1, FF_OWN), F32),
        jax.ShapeDtypeStruct((BLK, FF_OWN), F32),
    )
    results = pl.pallas_call(
        layer_kernel,
        out_shape=shapes,
        in_specs=[pl.BlockSpec(memory_space=pltpu.SMEM)] + [vspec] * 10,
        out_specs=tuple([vspec] * 10),
        scratch_shapes=scratch,
        compiler_params=pltpu.CompilerParams(
            collective_id=0, has_side_effects=True, vmem_limit_bytes=62 * 2**20
        ),
        name="encoder_layer",
    )(
        image_count,
        tokens.reshape(rows, width),
        cotangent.reshape(rows, width),
        ln_gain,
        vec_bias,
        w_qkv,
        qv_bias,
        w_out,
        w_fc1,
        fc1_bias,
        w_fc2.T,
    )
    aspec = pl.BlockSpec(memory_space=pl.ANY)
    out, gtok, gains, biases, gqkv, gqv, gout, gfc1, gfc1b, gfc2 = pl.pallas_call(
        deliver,
        out_shape=shapes[:8] + (jax.ShapeDtypeStruct((FF_OWN,), F32),) + shapes[9:],
        in_specs=[aspec] * 10,
        out_specs=tuple([vspec] * 10),
        scratch_shapes=[pltpu.SemaphoreType.DMA((10,)), pltpu.VMEM((1, FF_OWN), F32)],
        name="deliver",
    )(*results)
    return (
        out.reshape(slots, rows, width),
        gtok.reshape(slots, rows, width),
        gains,
        biases,
        gqkv,
        gqv,
        gout,
        gfc1,
        gfc1b,
        gfc2.T,
    )


def solution(mesh):
    placed = (
        P("shard", "ctx", None),
        P("shard"),
        P(None, "shard"),
        P(None, "shard"),
        P(None, "shard", "tp"),
        P(None, "tp"),
        P("tp", "shard"),
        P("shard", "tp"),
        P("tp"),
        P("tp", "shard"),
        P("shard", "ctx", None),
    )
    return jax.shard_map(
        per_device,
        mesh=mesh,
        in_specs=placed,
        out_specs=(
            P("shard", "ctx", None),
            P("shard", "ctx", None),
            P(None, "shard"),
            P(None, "shard"),
            P(None, "shard", "tp"),
            P(None, "tp"),
            P("tp", "shard"),
            P("shard", "tp"),
            P("tp"),
            P("tp", "shard"),
        ),
        check_vma=False,
    )
```
